512 devices in a mesh: dp: 32 (over z_hi, x, core), proto: 16 (over z_lo, y).
Axes of the slice: x: 4, y: 4, z: 16 (z_hi: 4, z_lo: 4; z = z_hi * 4 + z_lo), core: 2. Of those that a mesh axis runs over, the one named last changes fastest.
Arguments:
- points: bfloat16 [65536, 768], P('dp'), may hold values from -6 to 6
- prototypes: bfloat16 [16384, 768], P('proto'), may hold values from -6 to 6
- plan_stride_lengths: float32 [3], replicated, may hold values from 1.5 to 5
- sigma_steps: float32 [3], replicated, may hold values from 0.2 to 1
Outputs:
- row_duals: float32 [65536], P('dp')
- col_duals: float32 [16384], P('proto')
- new_prototypes: float32 [16384, 768], P(('proto', 'dp'))
The draws below stay inside these ranges and needn't reach their ends.
All inputs are finite; a program needn't handle non-finite values.
Results may differ from the reference program's by a relative error of at most 0.0017.
Values sent between devices are 32-bit elements; how exact they have to be, the bound alone decides.
A program may use at most 64 MiB of HBM per device.

```python
import math
import jax
import jax.numpy as jnp
from jax import lax

LATENT_DIMENSION = 768
K = 16384
ITERS = 3
POINTS_PER_SHARD = 2048
NPTS = 65536


def shard_levels(own_key, shape, shards, least, largest):
    loudness, own = 1.0, jax.random.fold_in(own_key, 6)
    for axis_at, parts in shards:
        draws = jnp.exp(jax.random.uniform(jax.random.fold_in(own, axis_at), (parts,), jnp.float32, least / len(shards), largest / len(shards)))
        loudness = loudness * jnp.repeat(draws, shape[axis_at] // parts).reshape([-1 if axis == axis_at else 1 for axis in range(len(shape))])
    return loudness


def noise(own_key, dims, scale, bound, split=(), dtype=jnp.bfloat16):
    level = shard_levels(own_key, dims, split, -0.22, 0.18) if split else 1.0
    values = jax.random.normal(own_key, dims, jnp.float32) * scale * level
    return jnp.minimum(jnp.maximum(values, -bound), bound).astype(dtype)


def setup_inputs(seed: int = 0) -> dict:
    keys = jax.random.split(jax.random.key(seed), 5)
    points = noise(keys[0], (NPTS, LATENT_DIMENSION), 1.0, 6.0, ((0, 32),))
    prototypes = noise(keys[1], (K, LATENT_DIMENSION), 1.0, 6.0, ((0, 16),))
    plan_stride_lengths = jnp.clip(jnp.exp(jax.random.uniform(keys[2], (ITERS,), jnp.float32, math.log(1.5), math.log(5.0))), 1.5, 5.0)
    sigma_steps = jnp.clip(jnp.exp(jax.random.uniform(keys[3], (ITERS,), jnp.float32, math.log(0.2), math.log(1.0))), 0.2, 1.0)
    return dict(points=points, prototypes=prototypes, plan_stride_lengths=plan_stride_lengths, sigma_steps=sigma_steps)


sharpness_factor = 20.0

def unit_rows(values):
    wide = values.astype(jnp.float32)
    return (wide * lax.rsqrt(lax.optimization_barrier(jnp.mean(wide * wide, axis=1, keepdims=True)) + 1e-06)).astype(jnp.bfloat16)

def primal_update(transport, affinity_table, row_part, col_part, tau_value):
    return jnp.maximum(0.0, transport - tau_value / K * (row_part[:, None] + col_part[None, :] - affinity_table))

def reference(points, prototypes, plan_stride_lengths, sigma_steps):
    unit_protos = unit_rows(prototypes)
    block_count = NPTS // POINTS_PER_SHARD
    point_blocks = points.reshape(block_count, POINTS_PER_SHARD, LATENT_DIMENSION)
    col_target = NPTS / K

    def scores_of(block):
        unit_block = unit_rows(block)
        similarity_dotted = lax.dot_general(unit_block, unit_protos, (((1,), (1,)), ((), ())), preferred_element_type=jnp.float32)
        return similarity_dotted * (sharpness_factor / LATENT_DIMENSION)
    row_history = []
    col_history = []
    row_duals = jnp.zeros((NPTS,), jnp.float32)
    col_duals = jnp.zeros((K,), jnp.float32)

    def replay(affinity_table, row_stack, count):
        transport = jnp.zeros(affinity_table.shape, jnp.float32)
        for index in range(count):
            transport = primal_update(transport, affinity_table, row_stack[index], col_history_all[index], plan_stride_lengths[index])
        return transport
    for step_index in range(ITERS):
        col_history_all = col_history + [col_duals]
        piled_together = jnp.stack(row_history + [row_duals]).reshape(step_index + 1, block_count, POINTS_PER_SHARD)
        piled_together = jnp.transpose(piled_together, (1, 0, 2))

        def visit(col_total, inputs):
            block, row_stack = inputs
            affinity_table = scores_of(block)
            previous = replay(affinity_table, row_stack, step_index)
            fresh = primal_update(previous, affinity_table, row_stack[step_index], col_duals, plan_stride_lengths[step_index])
            extra = 2.0 * fresh - previous
            return (col_total + lax.optimization_barrier(jnp.sum(extra, axis=0)), lax.optimization_barrier(jnp.sum(extra, axis=1)))
        col_total, row_total = lax.scan(visit, jnp.zeros((K,), jnp.float32), (point_blocks, piled_together))
        row_history.append(row_duals)
        col_history.append(col_duals)
        row_duals = row_duals + sigma_steps[step_index] * (row_total.reshape(NPTS) - 1.0)
        col_duals = col_duals + sigma_steps[step_index] * (col_total - col_target)
    col_history_all = col_history
    piled_together = jnp.transpose(jnp.stack(row_history).reshape(ITERS, block_count, POINTS_PER_SHARD), (1, 0, 2))

    def finish(carry, inputs):
        refresh_aggregate, count_total = carry
        block, row_stack = inputs
        affinity_table = scores_of(block)
        transport = replay(affinity_table, row_stack, ITERS)
        plan_low = transport.astype(jnp.bfloat16)
        refresh_aggregate = refresh_aggregate + lax.dot_general(plan_low, block, (((0,), (0,)), ((), ())), preferred_element_type=jnp.float32)
        return ((refresh_aggregate, count_total + lax.optimization_barrier(jnp.sum(transport, axis=0))), None)
    start = (jnp.zeros((K, LATENT_DIMENSION), jnp.float32), jnp.zeros((K,), jnp.float32))
    (gathered, counts), unused = lax.scan(finish, start, (point_blocks, piled_together))
    new_prototypes = (prototypes.astype(jnp.float32) + gathered) / (1.0 + counts)[:, None]
    return (row_duals, col_duals, new_prototypes)
```

```python
import jax
import jax.numpy as jnp
from jax import lax
from jax.experimental import pallas as pl
from jax.experimental.pallas import tpu as pltpu
from jax.sharding import PartitionSpec as P

K = 16384
SHARPNESS = 20.0
MESH = pl.DeviceIdType.MESH

ZH, X, CORE, ZL, Y = 4, 4, 2, 4, 4
ROUNDS = 3
POINTS, PROTOS, WIDTH = 2048, 1024, 768
PCHUNK = 256
NCHUNK = POINTS // PCHUNK
LANES = POINTS // 128
GROUPS = PROTOS // 8
BLOCK = PROTOS // ZH
BGROUPS = BLOCK // 8
OUT = PROTOS // (ZH * X * CORE)
HALF = OUT // 2
ORDER = (2, 1, 3, 0)
F32, BF16 = jnp.float32, jnp.bfloat16


def unit_rows(values):
    wide = values.astype(F32)
    return (wide * lax.rsqrt(jnp.mean(wide * wide, axis=1, keepdims=True) + 1e-06)).astype(BF16)


def kernel(
    strides, sigmas, pts_hbm, protos_hbm,
    rowd_ref, cold_ref, newp_ref,
    pts, protos, uprot, a_ref, b_ref, plan, wr, wc, rowacc, colacc,
    ra, rb, ca, cb, part, corebuf, xmid, xend, total, zmid, zend, count_ref,
    in_sem, ra_s, ra_r, rb_s, rb_r, ca_s, ca_r, cb_s, cb_r, core_s, core_r, x_s, x_r, z_s, z_r,
):
    me_dp, me_pr = lax.axis_index("dp"), lax.axis_index("proto")
    zh, x, core = me_dp // (X * CORE), (me_dp // CORE) % X, me_dp % CORE
    xc = me_dp % (X * CORE)
    zl, y = me_pr // Y, me_pr % Y

    def at_xc(d):
        return (zh * (X * CORE) + d, me_pr)

    def at_x(d):
        return at_xc(((x + d + X) % X) * CORE + core)

    def at_zh(d):
        return (((zh + d + ZH) % ZH) * (X * CORE) + xc, me_pr)

    def at_y(d):
        return (me_dp, zl * Y + (y + d) % Y)

    def at_zl(d):
        return (me_dp, ((zl + d) % ZL) * Y + y)

    xc_peers = []
    for d in range(1, X * CORE):
        slot = ((x + d // CORE) % X) * CORE + (core + d % CORE) % CORE
        xc_peers.append((slot, at_xc(slot)))
    zh_peers = [((zh + d) % ZH, at_zh(d)) for d in range(1, ZH)]
    y_peers = [((y + d) % Y, at_y(d)) for d in range(1, Y)]
    zl_peers = [((zl + d) % ZL, at_zl(d)) for d in range(1, ZL)]
    everyone = xc_peers + zh_peers + y_peers + zl_peers

    barrier = pltpu.get_barrier_semaphore()
    for _, dev in everyone:
        pl.semaphore_signal(barrier, inc=1, device_id=dev, device_id_type=MESH)

    protos_in = pltpu.make_async_copy(protos_hbm, protos, in_sem.at[NCHUNK])
    protos_in.start()

    def pts_in(j):
        rows = pl.ds(j * PCHUNK, PCHUNK)
        return pltpu.make_async_copy(pts_hbm.at[rows], pts.at[rows], in_sem.at[j])

    for j in range(NCHUNK):
        pts_in(j).start()

    scale = SHARPNESS / WIDTH
    tau = [strides[t] / K for t in range(ROUNDS)]
    target = float(POINTS * ZH * X * CORE) / K

    pending = []

    def spread(buf, send, recv, t, mine, peers):
        for slot, dev in peers:
            copy = pltpu.make_async_remote_copy(
                src_ref=buf.at[t, mine], dst_ref=buf.at[t, mine],
                send_sem=send.at[t, slot], recv_sem=recv.at[t, mine],
                device_id=dev, device_id_type=MESH)
            copy.start()
            pending.append(copy)

    def gather(buf, send, recv, t, peers):
        for slot, dev in peers:
            pltpu.make_async_remote_copy(
                src_ref=buf.at[t, slot], dst_ref=buf.at[t, slot],
                send_sem=send.at[t, slot], recv_sem=recv.at[t, slot],
                device_id=dev, device_id_type=MESH).wait_recv()
        out = buf[t, 0]
        for slot in range(1, buf.shape[1]):
            out = out + buf[t, slot]
        return out

    def sums_out(t, factor):
        for g in range(PROTOS // 128):
            block = colacc[g * 16:(g + 1) * 16].reshape(128, 128)
            ca[t, xc, g:g + 1, :] = factor * jnp.sum(block.T, axis=0, keepdims=True)
        spread(ca, ca_s, ca_r, t, xc, xc_peers)
        for l in range(LANES):
            ra[t, y, l:l + 1, :] = factor * jnp.sum(rowacc[:, l * 128:(l + 1) * 128], axis=0, keepdims=True)
        spread(ra, ra_s, ra_r, t, y, y_peers)

    def sums_mid(t):
        cb[t, zh] = gather(ca, ca_s, ca_r, t, xc_peers)
        spread(cb, cb_s, cb_r, t, zh, zh_peers)
        rb[t, zl] = gather(ra, ra_s, ra_r, t, y_peers)
        spread(rb, rb_s, rb_r, t, zl, zl_peers)

    def sums_in(t):
        cols = gather(cb, cb_s, cb_r, t, zh_peers)
        rows = gather(rb, rb_s, rb_r, t, zl_peers)
        return rows, cols

    def duals_in(rowd, cold, step):
        tall = (step * cold).T
        for g in range(PROTOS // 128):
            wc[g * 16:(g + 1) * 16] = jnp.broadcast_to(tall[:, g:g + 1], (128, 128)).reshape(16, 8, 128)
        for l in range(LANES):
            wr[:, l * 128:(l + 1) * 128] = jnp.broadcast_to(step * rowd[l:l + 1, :], (8, 128))

    protos_in.wait()

    def unit_protos(i, carry):
        rows = pl.ds(pl.multiple_of(i * 128, 128), 128)
        uprot[rows, :] = unit_rows(protos[rows, :])
        return carry

    lax.fori_loop(0, PROTOS // 128, unit_protos, 0)
    colacc[...] = jnp.zeros_like(colacc)

    def scores(j, carry):
        pts_in(j).wait()
        first = pl.multiple_of(j * PCHUNK, PCHUNK)
        unit = unit_rows(pts[pl.ds(first, PCHUNK), :])
        s = lax.dot_general(uprot[...], unit, (((1,), (1,)), ((), ())), preferred_element_type=F32)
        s = s.reshape(GROUPS, 8, PCHUNK)
        a_ref[:, :, pl.ds(first, PCHUNK)] = s
        p = jnp.maximum(s, 0.0)
        rowacc[:, pl.ds(first, PCHUNK)] = jnp.sum(p, axis=0)
        part_sum = p[:, :, 0:128]
        for l in range(1, PCHUNK // 128):
            part_sum = part_sum + p[:, :, l * 128:(l + 1) * 128]
        colacc[...] += part_sum
        return carry

    lax.fori_loop(0, NCHUNK, scores, 0)
    pl.semaphore_wait(barrier, len(everyone))

    def first_plan(i, carry):
        rows = pl.ds(i * 4, 4)
        s = a_ref[rows]
        b_ref[rows] = jnp.maximum((tau[1] * scale) * s, ((tau[0] + tau[1]) * scale) * s)
        return carry

    def next_plan(i, carry):
        rows = pl.ds(i * 4, 4)
        b_ref[rows] = b_ref[rows] + (tau[2] * scale) * a_ref[rows]
        return carry

    def iterate(base, count, store):
        def step(i, carry):
            rows = pl.ds(base + i * 4, 4)
            c = wc[rows]
            acc = None
            for l in range(LANES):
                lanes = slice(l * 128, (l + 1) * 128)
                p = jnp.maximum(b_ref[rows, :, lanes] - (wr[:, lanes] + c), 0.0)
                rowacc[:, lanes] += jnp.sum(p, axis=0)
                acc = p if acc is None else acc + p
                store(i, rows, lanes, p)
            colacc[rows] = acc
            return carry

        lax.fori_loop(0, count, step, 0)

    sums_out(0, tau[0] * scale)
    lax.fori_loop(0, GROUPS // 8, first_plan, 0)
    sums_mid(0)
    lax.fori_loop(GROUPS // 8, GROUPS // 4, first_plan, 0)
    rows1, cols1 = sums_in(0)
    rowd = sigmas[0] * (2.0 * rows1 - 1.0)
    cold = sigmas[0] * (2.0 * cols1 - target)
    duals_in(rowd, cold, tau[1])

    rowacc[...] = jnp.zeros_like(rowacc)

    def keep(i, rows, lanes, p):
        b_ref[rows, :, lanes] = p

    iterate(0, GROUPS // 4, keep)
    sums_out(1, 1.0)
    lax.fori_loop(0, GROUPS // 8, next_plan, 0)
    sums_mid(1)
    lax.fori_loop(GROUPS // 8, GROUPS // 4, next_plan, 0)
    rows2, cols2 = sums_in(1)
    rowd = rowd + sigmas[1] * (2.0 * rows2 - rows1 - 1.0)
    cold = cold + sigmas[1] * (2.0 * cols2 - cols1 - target)
    duals_in(rowd, cold, tau[2])

    rowacc[...] = jnp.zeros_like(rowacc)
    other = 1 - core

    def remote(src, dst, sems, index, dev):
        return pltpu.make_async_remote_copy(
            src_ref=src, dst_ref=dst, send_sem=sems[0].at[index], recv_sem=sems[1].at[index],
            device_id=dev, device_id_type=MESH)

    core_sems, x_sems, z_sems = (core_s, core_r), (x_s, x_r), (z_s, z_r)
    peer = at_xc(x * CORE + other)

    def go(copy):
        copy.start()
        pending.append(copy)
        return copy

    def compute(c):
        base = ((zh + ORDER[c]) % ZH) * BGROUPS

        def low(i, rows, lanes, p):
            plan[pl.ds(pl.multiple_of(i * 32, 32), 32), lanes] = p.reshape(32, 128).astype(BF16)

        iterate(base, BGROUPS // 4, low)
        for n in range(WIDTH // 256):
            lanes = slice(n * 256, (n + 1) * 256)
            g = jnp.dot(plan[...], pts[:, lanes], preferred_element_type=F32)
            part[c, :, :, :, lanes] = g.reshape(X, CORE, OUT, 256)
        return go(remote(part.at[c, :, other], corebuf.at[c], core_sems, c, peer))

    right, left = at_x(1), at_x(-1)
    up, down = at_zh(1), at_zh(-1)
    xp, xm, xo = (x + 1) % X, (x + X - 1) % X, (x + 2) % X
    lo, hi = pl.ds(0, HALF), pl.ds(HALF, HALF)

    def x_first(c, core_copy):
        core_copy.wait_recv()
        part[c, xo, core] += corebuf[c, xo]
        far = [
            go(remote(part.at[c, xo, core, lo], xmid.at[c, 0], x_sems, (c, 0), right)),
            go(remote(part.at[c, xo, core, hi], xmid.at[c, 1], x_sems, (c, 1), left)),
        ]
        part[c, xp, core] += corebuf[c, xp]
        part[c, xm, core] += corebuf[c, xm]
        near = [
            go(remote(part.at[c, xp, core, hi], xend.at[c, 0, hi], x_sems, (c, 2), right)),
            go(remote(part.at[c, xm, core, lo], xend.at[c, 1, lo], x_sems, (c, 3), left)),
        ]
        part[c, x, core] += corebuf[c, x]
        return far, near

    def x_second(c, copies):
        far, near = copies
        far[0].wait_recv()
        part[c, xp, core, lo] += xmid[c, 0]
        near.append(go(remote(part.at[c, xp, core, lo], xend.at[c, 0, lo], x_sems, (c, 4), right)))
        far[1].wait_recv()
        part[c, xm, core, hi] += xmid[c, 1]
        near.append(go(remote(part.at[c, xm, core, hi], xend.at[c, 1, hi], x_sems, (c, 5), left)))
        return near

    def x_last(c, near):
        for copy in near:
            copy.wait_recv()
        total[c] = part[c, x, core] + xend[c, 0] + xend[c, 1]

    k0 = compute(0)
    k1 = compute(1)
    x0 = x_first(0, k0)
    k2 = compute(2)
    x1 = x_first(1, k1)
    x0 = x_second(0, x0)
    k3 = compute(3)
    x2 = x_first(2, k2)
    sums_out(2, 1.0)
    x1 = x_second(1, x1)
    x3 = x_first(3, k3)
    x_last(0, x0)
    zfar = [
        go(remote(total.at[0, lo], zmid.at[0], z_sems, 0, up)),
        go(remote(total.at[0, hi], zmid.at[1], z_sems, 1, down)),
    ]
    sums_mid(2)
    x2 = x_second(2, x2)
    x_last(1, x1)
    znear = [go(remote(total.at[1, hi], zend.at[0, hi], z_sems, 2, up))]
    x3 = x_second(3, x3)
    x_last(2, x2)
    znear.append(go(remote(total.at[2, lo], zend.at[1, lo], z_sems, 3, down)))
    zfar[0].wait_recv()
    total[1, lo] += zmid[0]
    znear.append(go(remote(total.at[1, lo], zend.at[0, lo], z_sems, 4, up)))
    zfar[1].wait_recv()
    total[2, hi] += zmid[1]
    znear.append(go(remote(total.at[2, hi], zend.at[1, hi], z_sems, 5, down)))
    rows3, cols3 = sums_in(2)
    rowd_ref[...] = rowd + sigmas[2] * (2.0 * rows3 - rows2 - 1.0)
    cold_ref[...] = cold + sigmas[2] * (2.0 * cols3 - cols2 - target)
    count_ref[...] = cols3
    mine = count_ref[pl.ds(me_dp // 4, 1), :]
    sub = lax.broadcasted_iota(jnp.int32, (OUT, 128), 0)
    lane = lax.broadcasted_iota(jnp.int32, (OUT, 128), 1)
    counts = jnp.sum(jnp.where(lane == sub + (me_dp % 4) * OUT, mine, 0.0), axis=1, keepdims=True)
    previous = protos[pl.ds(pl.multiple_of(me_dp * OUT, OUT), OUT), :].astype(F32)
    x_last(3, x3)
    for copy in znear:
        copy.wait_recv()
    gathered = total[3] + zend[0] + zend[1]
    newp_ref[...] = (previous + gathered) / (1.0 + counts)
    for copy in pending:
        copy.wait_send()


def body(points, prototypes, plan_stride_lengths, sigma_steps):
    dma = pltpu.SemaphoreType.DMA
    vmem = pl.BlockSpec(memory_space=pltpu.VMEM)
    smem = pl.BlockSpec(memory_space=pltpu.SMEM)
    hbm = pl.BlockSpec(memory_space=pl.ANY)
    rows, cols, new = pl.pallas_call(
        kernel,
        out_shape=(
            jax.ShapeDtypeStruct((LANES, 128), F32),
            jax.ShapeDtypeStruct((PROTOS // 128, 128), F32),
            jax.ShapeDtypeStruct((OUT, WIDTH), F32),
        ),
        in_specs=[smem, smem, hbm, hbm],
        out_specs=(vmem, vmem, vmem),
        scratch_shapes=[
            pltpu.VMEM((POINTS, WIDTH), BF16),
            pltpu.VMEM((PROTOS, WIDTH), BF16),
            pltpu.VMEM((PROTOS, WIDTH), BF16),
            pltpu.VMEM((GROUPS, 8, POINTS), F32),
            pltpu.VMEM((GROUPS, 8, POINTS), F32),
            pltpu.VMEM((BLOCK, POINTS), BF16),
            pltpu.VMEM((8, POINTS), F32),
            pltpu.VMEM((GROUPS, 8, 128), F32),
            pltpu.VMEM((8, POINTS), F32),
            pltpu.VMEM((GROUPS, 8, 128), F32),
            pltpu.VMEM((ROUNDS, Y, LANES, 128), F32),
            pltpu.VMEM((ROUNDS, ZL, LANES, 128), F32),
            pltpu.VMEM((ROUNDS, X * CORE, PROTOS // 128, 128), F32),
            pltpu.VMEM((ROUNDS, ZH, PROTOS // 128, 128), F32),
            pltpu.VMEM((ZH, X, CORE, OUT, WIDTH), F32),
            pltpu.VMEM((ZH, X, OUT, WIDTH), F32),
            pltpu.VMEM((ZH, 2, HALF, WIDTH), F32),
            pltpu.VMEM((ZH, 2, OUT, WIDTH), F32),
            pltpu.VMEM((ZH, OUT, WIDTH), F32),
            pltpu.VMEM((2, HALF, WIDTH), F32),
            pltpu.VMEM((2, OUT, WIDTH), F32),
            pltpu.VMEM((PROTOS // 128, 128), F32),
            dma((NCHUNK + 1,)),
            dma((ROUNDS, Y)), dma((ROUNDS, Y)),
            dma((ROUNDS, ZL)), dma((ROUNDS, ZL)),
            dma((ROUNDS, X * CORE)), dma((ROUNDS, X * CORE)),
            dma((ROUNDS, ZH)), dma((ROUNDS, ZH)),
            dma((ZH,)), dma((ZH,)),
            dma((ZH, 6)), dma((ZH, 6)),
            dma((6,)), dma((6,)),
        ],
        compiler_params=pltpu.CompilerParams(
            collective_id=0, has_side_effects=True, vmem_limit_bytes=56 * 1024 * 1024),
        name="assign",
    )(plan_stride_lengths, sigma_steps, points, prototypes)
    return rows.reshape(POINTS), cols.reshape(PROTOS), new


def solution(mesh):
    placed = (P("dp", None), P("proto", None), P(), P())
    return jax.shard_map(
        body,
        mesh=mesh,
        in_specs=placed,
        out_specs=(P("dp"), P("proto"), P(("proto", "dp"), None)),
        check_vma=False,
    )
```

```python
import jax
import jax.numpy as jnp
from jax import lax
from jax.experimental import pallas as pl
from jax.experimental.pallas import tpu as pltpu
from jax.sharding import PartitionSpec as P

K = 16384
SHARPNESS = 20.0
MESH = pl.DeviceIdType.MESH

ZH, X, CORE, ZL, Y = 4, 4, 2, 4, 4
ROUNDS = 3
POINTS, PROTOS, WIDTH = 2048, 1024, 768
PCHUNK = 512
NCHUNK = POINTS // PCHUNK
PHALF = PROTOS // 2
LANES = POINTS // 128
GROUPS = PROTOS // 8
BLOCK = PROTOS // ZH
BGROUPS = BLOCK // 8
OUT = PROTOS // (ZH * X * CORE)
HALF = OUT // 2
THIRDS = WIDTH // 256
F32, BF16 = jnp.float32, jnp.bfloat16


def unit_rows(values):
    wide = values.astype(F32)
    return (wide * lax.rsqrt(jnp.mean(wide * wide, axis=1, keepdims=True) + 1e-06)).astype(BF16)


def kernel(
    strides_hbm, sigmas_hbm, pts_hbm, protos_hbm,
    rowd_ref, cold_ref, newp_ref,
    strides, sigmas, pts, protos, upts, uprot, a_ref, b_ref, plan, wr, wc, rowacc, colacc,
    ra, rb, ca, cb, part, corebuf, xbuf, total, zmid, zend, count_ref,
    in_sem, ra_s, ra_r, rb_s, rb_r, ca_s, ca_r, cb_s, cb_r, core_s, core_r, x_s, x_r, far_s, far_r, near_s, near_r,
):
    me_dp, me_pr = lax.axis_index("dp"), lax.axis_index("proto")
    zh, x, core = me_dp // (X * CORE), (me_dp // CORE) % X, me_dp % CORE
    xc = me_dp % (X * CORE)
    zl, y = me_pr // Y, me_pr % Y

    def at_xc(d):
        return (zh * (X * CORE) + d, me_pr)

    def at_x(d):
        return at_xc(((x + d + X) % X) * CORE + core)

    def at_zh(d):
        return (((zh + d + ZH) % ZH) * (X * CORE) + xc, me_pr)

    def at_y(d):
        return (me_dp, zl * Y + (y + d) % Y)

    def at_zl(d):
        return (me_dp, ((zl + d) % ZL) * Y + y)

    xc_peers = []
    for d in range(1, X * CORE):
        slot = ((x + d // CORE) % X) * CORE + (core + d % CORE) % CORE
        xc_peers.append((slot, at_xc(slot)))
    zh_peers = [((zh + d) % ZH, at_zh(d)) for d in range(1, ZH)]
    y_peers = [((y + d) % Y, at_y(d)) for d in range(1, Y)]
    zl_peers = [((zl + d) % ZL, at_zl(d)) for d in range(1, ZL)]
    everyone = xc_peers + zh_peers + y_peers + zl_peers

    barrier = pltpu.get_barrier_semaphore()
    for _, dev in everyone:
        pl.semaphore_signal(barrier, inc=1, device_id=dev, device_id_type=MESH)

    def protos_in(h):
        rows = pl.ds(h * PHALF, PHALF)
        return pltpu.make_async_copy(protos_hbm.at[rows], protos.at[rows], in_sem.at[NCHUNK + h])

    def pts_in(j):
        rows = pl.ds(j * PCHUNK, PCHUNK)
        return pltpu.make_async_copy(pts_hbm.at[rows], pts.at[rows], in_sem.at[j])

    protos_in(0).start()
    for j in range(NCHUNK):
        pts_in(j).start()
    protos_in(1).start()
    strides_in = pltpu.make_async_copy(strides_hbm, strides, in_sem.at[NCHUNK + 2])
    sigmas_in = pltpu.make_async_copy(sigmas_hbm, sigmas, in_sem.at[NCHUNK + 3])
    strides_in.start()
    sigmas_in.start()

    scale = SHARPNESS / WIDTH
    target = float(POINTS * ZH * X * CORE) / K

    pending = []

    def spread(buf, send, recv, t, mine, peers):
        for slot, dev in peers:
            copy = pltpu.make_async_remote_copy(
                src_ref=buf.at[t, mine], dst_ref=buf.at[t, mine],
                send_sem=send.at[t, slot], recv_sem=recv.at[t, mine],
                device_id=dev, device_id_type=MESH)
            copy.start()
            pending.append(copy)

    def gather(buf, send, recv, t, peers):
        for slot, dev in peers:
            pltpu.make_async_remote_copy(
                src_ref=buf.at[t, slot], dst_ref=buf.at[t, slot],
                send_sem=send.at[t, slot], recv_sem=recv.at[t, slot],
                device_id=dev, device_id_type=MESH).wait_recv()
        out = buf[t, 0]
        for slot in range(1, buf.shape[1]):
            out = out + buf[t, slot]
        return out

    def sums_out(t, factor):
        for g in range(PROTOS // 128):
            block = colacc[g * 16:(g + 1) * 16].reshape(128, 128)
            ca[t, xc, g:g + 1, :] = factor * jnp.sum(block.T, axis=0, keepdims=True)
        spread(ca, ca_s, ca_r, t, xc, xc_peers)
        for l in range(LANES):
            ra[t, y, l:l + 1, :] = factor * jnp.sum(rowacc[:, l * 128:(l + 1) * 128], axis=0, keepdims=True)
        spread(ra, ra_s, ra_r, t, y, y_peers)

    def sums_mid(t):
        cb[t, zh] = gather(ca, ca_s, ca_r, t, xc_peers)
        spread(cb, cb_s, cb_r, t, zh, zh_peers)
        rb[t, zl] = gather(ra, ra_s, ra_r, t, y_peers)
        spread(rb, rb_s, rb_r, t, zl, zl_peers)

    def sums_in(t):
        cols = gather(cb, cb_s, cb_r, t, zh_peers)
        rows = gather(rb, rb_s, rb_r, t, zl_peers)
        return rows, cols

    def duals_in(rowd, cold, step):
        tall = (step * cold).T
        for g in range(PROTOS // 128):
            wc[g * 16:(g + 1) * 16] = jnp.broadcast_to(tall[:, g:g + 1], (128, 128)).reshape(16, 8, 128)
        for l in range(LANES):
            wr[:, l * 128:(l + 1) * 128] = jnp.broadcast_to(step * rowd[l:l + 1, :], (8, 128))

    strides_in.wait()
    sigmas_in.wait()
    tau = [strides[t] / K for t in range(ROUNDS)]
    colacc[...] = jnp.zeros_like(colacc)
    rowacc[...] = jnp.zeros_like(rowacc)

    def unit_protos(h):
        protos_in(h).wait()
        for i in range(PHALF // 128):
            rows = slice(h * PHALF + i * 128, h * PHALF + (i + 1) * 128)
            uprot[rows, :] = unit_rows(protos[rows, :])

    def unit_points(j):
        pts_in(j).wait()
        rows = slice(j * PCHUNK, (j + 1) * PCHUNK)
        upts[rows, :] = unit_rows(pts[rows, :])

    def scores(first, count, lanes, width):
        rows = pl.ds(pl.multiple_of(first, BLOCK), count)
        groups = pl.ds(first // 8, count // 8)
        s = lax.dot_general(uprot[rows, :], upts[lanes, :], (((1,), (1,)), ((), ())), preferred_element_type=F32)
        s = s.reshape(count // 8, 8, width)
        a_ref[groups, :, lanes] = s
        p = jnp.maximum(s, 0.0)
        rowacc[:, lanes] += jnp.sum(p, axis=0)
        acc = p[:, :, 0:128]
        for l in range(1, width // 128):
            acc = acc + p[:, :, l * 128:(l + 1) * 128]
        colacc[groups] += acc

    unit_protos(0)
    unit_points(0)
    for j in range(NCHUNK):
        scores(0, PHALF, slice(j * PCHUNK, (j + 1) * PCHUNK), PCHUNK)
        if j + 1 < NCHUNK:
            unit_points(j + 1)
    unit_protos(1)

    def rest(i, carry):
        scores(i * BLOCK, BLOCK, slice(0, POINTS), POINTS)
        return carry

    lax.fori_loop(PHALF // BLOCK, ZH, rest, 0)
    pl.semaphore_wait(barrier, len(everyone))

    def first_plan(i, carry):
        rows = pl.ds(i * 4, 4)
        s = a_ref[rows]
        b_ref[rows] = jnp.maximum((tau[1] * scale) * s, ((tau[0] + tau[1]) * scale) * s)
        return carry

    def next_plan(i, carry):
        rows = pl.ds(i * 4, 4)
        b_ref[rows] = b_ref[rows] + (tau[2] * scale) * a_ref[rows]
        return carry

    def iterate(base, count, store):
        def step(i, carry):
            rows = pl.ds(base + i * 8, 8)
            c = wc[rows]
            acc = None
            for l in range(LANES):
                lanes = slice(l * 128, (l + 1) * 128)
                p = jnp.maximum(b_ref[rows, :, lanes] - (wr[:, lanes] + c), 0.0)
                rowacc[:, lanes] += jnp.sum(p, axis=0)
                acc = p if acc is None else acc + p
                store(i, rows, lanes, p)
            colacc[rows] = acc
            return carry

        lax.fori_loop(0, count, step, 0)

    sums_out(0, tau[0] * scale)
    lax.fori_loop(0, GROUPS // 8, first_plan, 0)
    sums_mid(0)
    lax.fori_loop(GROUPS // 8, GROUPS // 4, first_plan, 0)
    rows1, cols1 = sums_in(0)
    rowd = sigmas[0] * (2.0 * rows1 - 1.0)
    cold = sigmas[0] * (2.0 * cols1 - target)
    duals_in(rowd, cold, tau[1])

    rowacc[...] = jnp.zeros_like(rowacc)

    def keep(i, rows, lanes, p):
        b_ref[rows, :, lanes] = p

    iterate(0, GROUPS // 8, keep)
    sums_out(1, 1.0)
    lax.fori_loop(0, GROUPS // 8, next_plan, 0)
    sums_mid(1)
    lax.fori_loop(GROUPS // 8, GROUPS // 4, next_plan, 0)
    rows2, cols2 = sums_in(1)
    rowd = rowd + sigmas[1] * (2.0 * rows2 - rows1 - 1.0)
    cold = cold + sigmas[1] * (2.0 * cols2 - cols1 - target)
    duals_in(rowd, cold, tau[2])

    rowacc[...] = jnp.zeros_like(rowacc)
    other = 1 - core
    peer = at_xc(x * CORE + other)
    right, left, across = at_x(1), at_x(-1), at_x(2)
    up, down = at_zh(1), at_zh(-1)
    xp, xm, xo = (x + 1) % X, (x + X - 1) % X, (x + 2) % X
    lo, hi = pl.ds(0, HALF), pl.ds(HALF, HALF)

    def remote(src, dst, send, recv, index, dev):
        return pltpu.make_async_remote_copy(
            src_ref=src, dst_ref=dst, send_sem=send.at[index], recv_sem=recv.at[index],
            device_id=dev, device_id_type=MESH)

    def core_copy(c, h):
        return remote(part.at[c, h, :, other], corebuf.at[c, h], core_s, core_r, (c, h), peer)

    def x_copy(c, h, n):
        to, dev = ((xp, right), (xm, left), (xo, across))[n]
        return remote(part.at[c, h, to, core], xbuf.at[c, h, n], x_s, x_r, (c, h, n), dev)

    def far_copy(h, n):
        rows, dev = ((lo, up), (hi, down))[n]
        return remote(total.at[0, h, rows], zmid.at[h, n], far_s, far_r, (h, n), dev)

    def near_copy(h, n, second):
        rows = (lo, hi)[n if second else 1 - n]
        return remote(total.at[1 + n, h, rows], zend.at[h, n, rows], near_s, near_r, (h, n, int(second)), (up, down)[n])

    def over_h(step):
        def loop(h, carry):
            step(h)
            return carry

        lax.fori_loop(0, THIRDS, loop, 0)

    def x_out(c, h):
        core_copy(c, h).wait_recv()
        for n in (2, 0, 1):
            to = (xp, xm, xo)[n]
            part[c, h, to, core] += corebuf[c, h, to]
            x_copy(c, h, n).start()

    def x_in(c, h):
        for n in range(X - 1):
            x_copy(c, h, n).wait_recv()
        total[c, h] = part[c, h, x, core] + corebuf[c, h, x] + (xbuf[c, h, 0] + xbuf[c, h, 1] + xbuf[c, h, 2])

    def plan_block(c, carry):
        second, odd = c // 2, c % 2
        base = ((zh + 2 + second - odd + 2 * second * odd) % ZH) * BGROUPS

        def low(i, rows, lanes, p):
            plan[c, pl.ds(pl.multiple_of(i * 64, 64), 64), lanes] = p.reshape(64, 128).astype(BF16)

        iterate(base, BGROUPS // 8, low)
        return carry

    def sums_block(c, carry):
        def third(h):
            lanes = pl.ds(pl.multiple_of(h * 256, 256), 256)
            g = jnp.dot(plan[c], pts[:, lanes], preferred_element_type=F32)
            part[c, h] = g.reshape(X, CORE, OUT, 256)
            core_copy(c, h).start()

        over_h(third)
        return carry

    lax.fori_loop(0, 1, plan_block, 0)
    lax.fori_loop(0, 1, sums_block, 0)
    lax.fori_loop(1, ZH, plan_block, 0)
    sums_out(2, 1.0)
    over_h(lambda h: x_out(0, h))
    lax.fori_loop(1, 3, sums_block, 0)

    def both_out(h):
        x_out(1, h)
        x_out(2, h)

    over_h(both_out)
    lax.fori_loop(3, ZH, sums_block, 0)
    sums_mid(2)
    over_h(lambda h: x_out(3, h))

    def far_out(h):
        x_in(0, h)
        for n in range(2):
            far_copy(h, n).start()

    over_h(far_out)

    def near_out(h):
        x_in(1, h)
        near_copy(h, 0, False).start()
        x_in(2, h)
        near_copy(h, 1, False).start()
        for n in range(2):
            rows = (lo, hi)[n]
            far_copy(h, n).wait_recv()
            total[1 + n, h, rows] += zmid[h, n]
            near_copy(h, n, True).start()

    over_h(near_out)
    rows3, cols3 = sums_in(2)
    rowd_ref[...] = rowd + sigmas[2] * (2.0 * rows3 - rows2 - 1.0)
    cold_ref[...] = cold + sigmas[2] * (2.0 * cols3 - cols2 - target)
    count_ref[...] = cols3
    mine = count_ref[pl.ds(me_dp // 4, 1), :]
    sub = lax.broadcasted_iota(jnp.int32, (OUT, 128), 0)
    lane = lax.broadcasted_iota(jnp.int32, (OUT, 128), 1)
    counts = jnp.sum(jnp.where(lane == sub + (me_dp % 4) * OUT, mine, 0.0), axis=1, keepdims=True)
    over_h(lambda h: x_in(3, h))
    for h in range(THIRDS):
        lanes = slice(h * 256, (h + 1) * 256)
        for n in range(2):
            for second in (False, True):
                near_copy(h, n, second).wait_recv()
        gathered = total[3, h] + (zend[h, 0] + zend[h, 1])
        previous = protos[pl.ds(pl.multiple_of(me_dp * OUT, OUT), OUT), lanes].astype(F32)
        newp_ref[:, lanes] = (previous + gathered) / (1.0 + counts)

    def sent(h):
        def blocks(c, carry):
            core_copy(c, h).wait_send()
            for n in range(X - 1):
                x_copy(c, h, n).wait_send()
            return carry

        lax.fori_loop(0, ZH, blocks, 0)
        for n in range(2):
            far_copy(h, n).wait_send()
            near_copy(h, n, False).wait_send()
            near_copy(h, n, True).wait_send()

    over_h(sent)
    for copy in pending:
        copy.wait_send()


def results(rows_in, cols_in, new_in, rows_out, cols_out, new_out):
    rows_out[...] = rows_in[...]
    cols_out[...] = cols_in[...]
    new_out[...] = new_in[...]


def body(points, prototypes, plan_stride_lengths, sigma_steps):
    dma = pltpu.SemaphoreType.DMA
    vmem = pl.BlockSpec(memory_space=pltpu.VMEM)
    hbm = pl.BlockSpec(memory_space=pl.ANY)
    rows, cols, new = pl.pallas_call(
        kernel,
        out_shape=(
            jax.ShapeDtypeStruct((LANES, 128), F32),
            jax.ShapeDtypeStruct((PROTOS // 128, 128), F32),
            jax.ShapeDtypeStruct((OUT, WIDTH), F32),
        ),
        in_specs=[hbm, hbm, hbm, hbm],
        out_specs=(vmem, vmem, vmem),
        scratch_shapes=[
            pltpu.SMEM((ROUNDS,), F32),
            pltpu.SMEM((ROUNDS,), F32),
            pltpu.VMEM((POINTS, WIDTH), BF16),
            pltpu.VMEM((PROTOS, WIDTH), BF16),
            pltpu.VMEM((POINTS, WIDTH), BF16),
            pltpu.VMEM((PROTOS, WIDTH), BF16),
            pltpu.VMEM((GROUPS, 8, POINTS), F32),
            pltpu.VMEM((GROUPS, 8, POINTS), F32),
            pltpu.VMEM((ZH, BLOCK, POINTS), BF16),
            pltpu.VMEM((8, POINTS), F32),
            pltpu.VMEM((GROUPS, 8, 128), F32),
            pltpu.VMEM((8, POINTS), F32),
            pltpu.VMEM((GROUPS, 8, 128), F32),
            pltpu.VMEM((ROUNDS, Y, LANES, 128), F32),
            pltpu.VMEM((ROUNDS, ZL, LANES, 128), F32),
            pltpu.VMEM((ROUNDS, X * CORE, PROTOS // 128, 128), F32),
            pltpu.VMEM((ROUNDS, ZH, PROTOS // 128, 128), F32),
            pltpu.VMEM((ZH, THIRDS, X, CORE, OUT, 256), F32),
            pltpu.VMEM((ZH, THIRDS, X, OUT, 256), F32),
            pltpu.VMEM((ZH, THIRDS, X - 1, OUT, 256), F32),
            pltpu.VMEM((ZH, THIRDS, OUT, 256), F32),
            pltpu.VMEM((THIRDS, 2, HALF, 256), F32),
            pltpu.VMEM((THIRDS, 2, OUT, 256), F32),
            pltpu.VMEM((PROTOS // 128, 128), F32),
            dma((NCHUNK + 4,)),
            dma((ROUNDS, Y)), dma((ROUNDS, Y)),
            dma((ROUNDS, ZL)), dma((ROUNDS, ZL)),
            dma((ROUNDS, X * CORE)), dma((ROUNDS, X * CORE)),
            dma((ROUNDS, ZH)), dma((ROUNDS, ZH)),
            dma((ZH, THIRDS)), dma((ZH, THIRDS)),
            dma((ZH, THIRDS, X - 1)), dma((ZH, THIRDS, X - 1)),
            dma((THIRDS, 2)), dma((THIRDS, 2)),
            dma((THIRDS, 2, 2)), dma((THIRDS, 2, 2)),
        ],
        compiler_params=pltpu.CompilerParams(
            collective_id=0, has_side_effects=True, vmem_limit_bytes=56 * 1024 * 1024),
        name="assign",
    )(plan_stride_lengths, sigma_steps, points, prototypes)
    rows, cols, new = pl.pallas_call(
        results,
        out_shape=(
            jax.ShapeDtypeStruct((LANES, 128), F32),
            jax.ShapeDtypeStruct((PROTOS // 128, 128), F32),
            jax.ShapeDtypeStruct((OUT, WIDTH), F32),
        ),
        in_specs=[vmem, vmem, vmem],
        out_specs=(vmem, vmem, vmem),
        name="results",
    )(rows, cols, new)
    return rows.reshape(POINTS), cols.reshape(PROTOS), new


def solution(mesh):
    placed = (P("dp", None), P("proto", None), P(), P())
    return jax.shard_map(
        body,
        mesh=mesh,
        in_specs=placed,
        out_specs=(P("dp"), P("proto"), P(("proto", "dp"), None)),
        check_vma=False,
    )
```

```python
import jax
import jax.numpy as jnp
from jax import lax
from jax.experimental import pallas as pl
from jax.experimental.pallas import tpu as pltpu
from jax.sharding import PartitionSpec as P

K = 16384
SHARPNESS = 20.0
MESH = pl.DeviceIdType.MESH

ZH, X, CORE, ZL, Y = 4, 4, 2, 4, 4
ROUNDS = 3
POINTS, PROTOS, WIDTH = 2048, 1024, 768
PCHUNK = 512
NCHUNK = POINTS // PCHUNK
PHALF = PROTOS // 2
LANES = POINTS // 128
GROUPS = PROTOS // 8
BLOCK = PROTOS // ZH
BGROUPS = BLOCK // 8
OUT = PROTOS // (ZH * X * CORE)
HALF = OUT // 2
THIRDS = WIDTH // 256
F32, BF16 = jnp.float32, jnp.bfloat16


def unit_rows(values):
    wide = values.astype(F32)
    return (wide * lax.rsqrt(jnp.mean(wide * wide, axis=1, keepdims=True) + 1e-06)).astype(BF16)


def kernel(
    strides_hbm, sigmas_hbm, pts_hbm, protos_hbm,
    rowd_ref, cold_ref, newp_ref,
    strides, sigmas, pts, protos, upts, uprot, a_ref, b_ref, plan, wr, wc, rowacc, colacc,
    ra, rb, ca, cf, cb, part, corebuf, xbuf, total, zmid, zend, count_ref,
    in_sem, ra_s, ra_r, rb_s, rb_r, ca_s, ca_r, cf_s, cf_r, cb_s, cb_r, core_s, core_r, x_s, x_r, far_s, far_r, near_s, near_r,
):
    me_dp, me_pr = lax.axis_index("dp"), lax.axis_index("proto")
    zh, x, core = me_dp // (X * CORE), (me_dp // CORE) % X, me_dp % CORE
    xc = me_dp % (X * CORE)
    zl, y = me_pr // Y, me_pr % Y

    def at_xc(d):
        return (zh * (X * CORE) + d, me_pr)

    def at_x(d):
        return at_xc(((x + d + X) % X) * CORE + core)

    def at_zh(d):
        return (((zh + d + ZH) % ZH) * (X * CORE) + xc, me_pr)

    def at_y(d):
        return (me_dp, zl * Y + (y + d) % Y)

    def at_zl(d):
        return (me_dp, ((zl + d) % ZL) * Y + y)

    xc_peers = []
    for d in range(1, X * CORE):
        slot = ((x + d // CORE) % X) * CORE + (core + d % CORE) % CORE
        xc_peers.append((slot, at_xc(slot)))
    far_peers = []
    for d in range(X * CORE):
        slot = ((x + d // CORE) % X) * CORE + (core + d % CORE) % CORE
        far_peers.append((slot, (((zh + 2) % ZH) * (X * CORE) + slot, me_pr)))
    zh_peers = [((zh + d) % ZH, at_zh(d)) for d in (1, ZH - 1)]
    y_peers = [((y + d) % Y, at_y(d)) for d in range(1, Y)]
    zl_peers = [((zl + d) % ZL, at_zl(d)) for d in range(1, ZL)]
    everyone = xc_peers + far_peers + zh_peers + y_peers + zl_peers

    barrier = pltpu.get_barrier_semaphore()
    for _, dev in everyone:
        pl.semaphore_signal(barrier, inc=1, device_id=dev, device_id_type=MESH)

    def protos_in(h):
        rows = pl.ds(h * PHALF, PHALF)
        return pltpu.make_async_copy(protos_hbm.at[rows], protos.at[rows], in_sem.at[NCHUNK + h])

    def pts_in(j):
        rows = pl.ds(j * PCHUNK, PCHUNK)
        return pltpu.make_async_copy(pts_hbm.at[rows], pts.at[rows], in_sem.at[j])

    protos_in(0).start()
    for j in range(NCHUNK):
        pts_in(j).start()
    protos_in(1).start()
    strides_in = pltpu.make_async_copy(strides_hbm, strides, in_sem.at[NCHUNK + 2])
    sigmas_in = pltpu.make_async_copy(sigmas_hbm, sigmas, in_sem.at[NCHUNK + 3])
    strides_in.start()
    sigmas_in.start()

    scale = SHARPNESS / WIDTH
    target = float(POINTS * ZH * X * CORE) / K

    pending = []

    def spread(buf, send, recv, t, mine, peers):
        for slot, dev in peers:
            copy = pltpu.make_async_remote_copy(
                src_ref=buf.at[t, mine], dst_ref=buf.at[t, mine],
                send_sem=send.at[t, slot], recv_sem=recv.at[t, mine],
                device_id=dev, device_id_type=MESH)
            copy.start()
            pending.append(copy)

    def far_group(t, slot, dev):
        return pltpu.make_async_remote_copy(
            src_ref=ca.at[t, xc], dst_ref=cf.at[t, xc],
            send_sem=cf_s.at[t, slot], recv_sem=cf_r.at[t, xc],
            device_id=dev, device_id_type=MESH)

    def total_of(buf, t):
        out = buf[t, 0]
        for slot in range(1, buf.shape[1]):
            out = out + buf[t, slot]
        return out

    def gather(buf, send, recv, t, peers):
        for slot, dev in peers:
            pltpu.make_async_remote_copy(
                src_ref=buf.at[t, slot], dst_ref=buf.at[t, slot],
                send_sem=send.at[t, slot], recv_sem=recv.at[t, slot],
                device_id=dev, device_id_type=MESH).wait_recv()
        return total_of(buf, t)

    def sums_out(t, factor):
        for g in range(PROTOS // 128):
            block = colacc[g * 16:(g + 1) * 16].reshape(128, 128)
            ca[t, xc, g:g + 1, :] = factor * jnp.sum(block.T, axis=0, keepdims=True)
        for slot, dev in far_peers:
            copy = far_group(t, slot, dev)
            copy.start()
            pending.append(copy)
        spread(ca, ca_s, ca_r, t, xc, xc_peers)
        for l in range(LANES):
            ra[t, y, l:l + 1, :] = factor * jnp.sum(rowacc[:, l * 128:(l + 1) * 128], axis=0, keepdims=True)
        spread(ra, ra_s, ra_r, t, y, y_peers)

    def sums_mid(t):
        cb[t, zh] = gather(ca, ca_s, ca_r, t, xc_peers)
        spread(cb, cb_s, cb_r, t, zh, zh_peers)
        rb[t, zl] = gather(ra, ra_s, ra_r, t, y_peers)
        spread(rb, rb_s, rb_r, t, zl, zl_peers)

    def rows_in(t):
        return gather(rb, rb_s, rb_r, t, zl_peers)

    def cols_in(t):
        for slot, dev in far_peers:
            pltpu.make_async_remote_copy(
                src_ref=ca.at[t, xc], dst_ref=cf.at[t, slot],
                send_sem=cf_s.at[t, slot], recv_sem=cf_r.at[t, slot],
                device_id=dev, device_id_type=MESH).wait_recv()
        cb[t, (zh + 2) % ZH] = total_of(cf, t)
        return gather(cb, cb_s, cb_r, t, zh_peers)

    def rowd_in(rowd, step):
        for l in range(LANES):
            wr[:, l * 128:(l + 1) * 128] = jnp.broadcast_to(step * rowd[l:l + 1, :], (8, 128))

    def cold_in(cold, step):
        tall = (step * cold).T
        for g in range(PROTOS // 128):
            wc[g * 16:(g + 1) * 16] = jnp.broadcast_to(tall[:, g:g + 1], (128, 128)).reshape(16, 8, 128)

    strides_in.wait()
    sigmas_in.wait()
    tau = [strides[t] / K for t in range(ROUNDS)]
    colacc[...] = jnp.zeros_like(colacc)
    rowacc[...] = jnp.zeros_like(rowacc)

    def unit_protos(h):
        protos_in(h).wait()
        for i in range(PHALF // 128):
            rows = slice(h * PHALF + i * 128, h * PHALF + (i + 1) * 128)
            uprot[rows, :] = unit_rows(protos[rows, :])

    def unit_points(j):
        pts_in(j).wait()
        rows = slice(j * PCHUNK, (j + 1) * PCHUNK)
        upts[rows, :] = unit_rows(pts[rows, :])

    def scores(first, count, lanes, width):
        rows = pl.ds(pl.multiple_of(first, BLOCK), count)
        groups = pl.ds(first // 8, count // 8)
        s = lax.dot_general(uprot[rows, :], upts[lanes, :], (((1,), (1,)), ((), ())), preferred_element_type=F32)
        s = s.reshape(count // 8, 8, width)
        a_ref[groups, :, lanes] = s
        p = jnp.maximum(s, 0.0)
        rowacc[:, lanes] += jnp.sum(p, axis=0)
        acc = p[:, :, 0:128]
        for l in range(1, width // 128):
            acc = acc + p[:, :, l * 128:(l + 1) * 128]
        colacc[groups] += acc

    unit_protos(0)
    unit_points(0)
    for j in range(NCHUNK):
        scores(0, PHALF, slice(j * PCHUNK, (j + 1) * PCHUNK), PCHUNK)
        if j + 1 < NCHUNK:
            unit_points(j + 1)
    unit_protos(1)

    def rest(i, carry):
        scores(i * BLOCK, BLOCK, slice(0, POINTS), POINTS)
        return carry

    lax.fori_loop(PHALF // BLOCK, ZH, rest, 0)
    pl.semaphore_wait(barrier, len(everyone))

    def first_plan(i, carry):
        rows = pl.ds(i * 4, 4)
        s = a_ref[rows]
        b_ref[rows] = jnp.maximum((tau[1] * scale) * s, ((tau[0] + tau[1]) * scale) * s)
        return carry

    def next_plan(i, carry):
        rows = pl.ds(i * 4, 4)
        b_ref[rows] = b_ref[rows] + (tau[2] * scale) * a_ref[rows]
        return carry

    def iterate(base, count, store):
        def step(i, carry):
            rows = pl.ds(base + i * 8, 8)
            c = wc[rows]
            acc = None
            for l in range(LANES):
                lanes = slice(l * 128, (l + 1) * 128)
                p = jnp.maximum(b_ref[rows, :, lanes] - (wr[:, lanes] + c), 0.0)
                rowacc[:, lanes] += jnp.sum(p, axis=0)
                acc = p if acc is None else acc + p
                store(i, rows, lanes, p)
            colacc[rows] = acc
            return carry

        lax.fori_loop(0, count, step, 0)

    sums_out(0, tau[0] * scale)
    lax.fori_loop(0, GROUPS // 8, first_plan, 0)
    sums_mid(0)
    lax.fori_loop(GROUPS // 8, GROUPS // 4, first_plan, 0)
    rowacc[...] = jnp.zeros_like(rowacc)
    rows1 = rows_in(0)
    rowd = sigmas[0] * (2.0 * rows1 - 1.0)
    rowd_in(rowd, tau[1])
    cols1 = cols_in(0)
    cold = sigmas[0] * (2.0 * cols1 - target)
    cold_in(cold, tau[1])


    def keep(i, rows, lanes, p):
        b_ref[rows, :, lanes] = p

    iterate(0, GROUPS // 8, keep)
    sums_out(1, 1.0)
    lax.fori_loop(0, GROUPS // 8, next_plan, 0)
    sums_mid(1)
    lax.fori_loop(GROUPS // 8, GROUPS // 4, next_plan, 0)
    rowacc[...] = jnp.zeros_like(rowacc)
    rows2 = rows_in(1)
    rowd = rowd + sigmas[1] * (2.0 * rows2 - rows1 - 1.0)
    rowd_in(rowd, tau[2])
    cols2 = cols_in(1)
    cold = cold + sigmas[1] * (2.0 * cols2 - cols1 - target)
    cold_in(cold, tau[2])

    other = 1 - core
    peer = at_xc(x * CORE + other)
    right, left, across = at_x(1), at_x(-1), at_x(2)
    up, down = at_zh(1), at_zh(-1)
    xp, xm, xo = (x + 1) % X, (x + X - 1) % X, (x + 2) % X
    lo, hi = pl.ds(0, HALF), pl.ds(HALF, HALF)

    def remote(src, dst, send, recv, index, dev):
        return pltpu.make_async_remote_copy(
            src_ref=src, dst_ref=dst, send_sem=send.at[index], recv_sem=recv.at[index],
            device_id=dev, device_id_type=MESH)

    def core_copy(c, h):
        return remote(part.at[c, h, :, other], corebuf.at[c, h], core_s, core_r, (c, h), peer)

    def x_copy(c, h, n):
        to, dev = ((xp, right), (xm, left), (xo, across))[n]
        return remote(part.at[c, h, to, core], xbuf.at[c, h, n], x_s, x_r, (c, h, n), dev)

    def far_copy(h, n):
        rows, dev = ((lo, up), (hi, down))[n]
        return remote(total.at[0, h, rows], zmid.at[h, n], far_s, far_r, (h, n), dev)

    def near_copy(h, n, second):
        rows = (lo, hi)[n if second else 1 - n]
        return remote(total.at[1 + n, h, rows], zend.at[h, n, rows], near_s, near_r, (h, n, int(second)), (up, down)[n])

    def over_h(step):
        def loop(h, carry):
            step(h)
            return carry

        lax.fori_loop(0, THIRDS, loop, 0)

    def x_out(c, h):
        core_copy(c, h).wait_recv()
        for n in (2, 0, 1):
            to = (xp, xm, xo)[n]
            part[c, h, to, core] += corebuf[c, h, to]
            x_copy(c, h, n).start()

    def x_in(c, h):
        for n in range(X - 1):
            x_copy(c, h, n).wait_recv()
        total[c, h] = part[c, h, x, core] + corebuf[c, h, x] + (xbuf[c, h, 0] + xbuf[c, h, 1] + xbuf[c, h, 2])

    def plan_block(c, carry):
        second, odd = c // 2, c % 2
        base = ((zh + 2 + second - odd + 2 * second * odd) % ZH) * BGROUPS

        def low(i, rows, lanes, p):
            plan[c, pl.ds(pl.multiple_of(i * 64, 64), 64), lanes] = p.reshape(64, 128).astype(BF16)

        iterate(base, BGROUPS // 8, low)
        return carry

    def sums_block(c, carry):
        def third(h):
            lanes = pl.ds(pl.multiple_of(h * 256, 256), 256)
            g = jnp.dot(plan[c], pts[:, lanes], preferred_element_type=F32)
            part[c, h] = g.reshape(X, CORE, OUT, 256)
            core_copy(c, h).start()

        over_h(third)
        return carry

    lax.fori_loop(0, 1, plan_block, 0)
    lax.fori_loop(0, 1, sums_block, 0)
    lax.fori_loop(1, 2, plan_block, 0)
    x_out(0, 0)
    x_out(0, 1)
    lax.fori_loop(2, ZH, plan_block, 0)
    sums_out(2, 1.0)
    x_out(0, 2)
    lax.fori_loop(1, 3, sums_block, 0)
    x_out(1, 0)
    x_out(2, 0)
    x_out(1, 1)
    lax.fori_loop(3, ZH, sums_block, 0)

    def far_out(h):
        x_in(0, h)
        for n in range(2):
            far_copy(h, n).start()
        x_out(2 - h % 2, 1 + (h + 1) // 2)

    over_h(far_out)
    sums_mid(2)

    def near_out(h):
        x_in(1, h)
        near_copy(h, 0, False).start()

        @pl.when(h < 2)
        def _():
            x_out(3, 2 * h)

        x_in(2, h)
        near_copy(h, 1, False).start()

        @pl.when(h == 0)
        def _():
            x_out(3, 1)

        for n in range(2):
            rows = (lo, hi)[n]
            far_copy(h, n).wait_recv()
            total[1 + n, h, rows] += zmid[h, n]
            near_copy(h, n, True).start()

    over_h(near_out)
    over_h(lambda h: x_in(3, h))
    rows3 = rows_in(2)
    cols3 = cols_in(2)
    rowd_ref[...] = rowd + sigmas[2] * (2.0 * rows3 - rows2 - 1.0)
    cold_ref[...] = cold + sigmas[2] * (2.0 * cols3 - cols2 - target)
    count_ref[...] = cols3
    mine = count_ref[pl.ds(me_dp // 4, 1), :]
    sub = lax.broadcasted_iota(jnp.int32, (OUT, 128), 0)
    lane = lax.broadcasted_iota(jnp.int32, (OUT, 128), 1)
    counts = jnp.sum(jnp.where(lane == sub + (me_dp % 4) * OUT, mine, 0.0), axis=1, keepdims=True)
    for h in range(THIRDS):
        lanes = slice(h * 256, (h + 1) * 256)
        for n in range(2):
            for second in (False, True):
                near_copy(h, n, second).wait_recv()
        gathered = total[3, h] + (zend[h, 0] + zend[h, 1])
        previous = protos[pl.ds(pl.multiple_of(me_dp * OUT, OUT), OUT), lanes].astype(F32)
        newp_ref[:, lanes] = (previous + gathered) / (1.0 + counts)

    def sent(h):
        def blocks(c, carry):
            core_copy(c, h).wait_send()
            for n in range(X - 1):
                x_copy(c, h, n).wait_send()
            return carry

        lax.fori_loop(0, ZH, blocks, 0)
        for n in range(2):
            far_copy(h, n).wait_send()
            near_copy(h, n, False).wait_send()
            near_copy(h, n, True).wait_send()

    over_h(sent)
    for copy in pending:
        copy.wait_send()


def results(rows_in, cols_in, new_in, rows_out, cols_out, new_out):
    rows_out[...] = rows_in[...]
    cols_out[...] = cols_in[...]
    new_out[...] = new_in[...]


def body(points, prototypes, plan_stride_lengths, sigma_steps):
    dma = pltpu.SemaphoreType.DMA
    vmem = pl.BlockSpec(memory_space=pltpu.VMEM)
    hbm = pl.BlockSpec(memory_space=pl.ANY)
    rows, cols, new = pl.pallas_call(
        kernel,
        out_shape=(
            jax.ShapeDtypeStruct((LANES, 128), F32),
            jax.ShapeDtypeStruct((PROTOS // 128, 128), F32),
            jax.ShapeDtypeStruct((OUT, WIDTH), F32),
        ),
        in_specs=[hbm, hbm, hbm, hbm],
        out_specs=(vmem, vmem, vmem),
        scratch_shapes=[
            pltpu.SMEM((ROUNDS,), F32),
            pltpu.SMEM((ROUNDS,), F32),
            pltpu.VMEM((POINTS, WIDTH), BF16),
            pltpu.VMEM((PROTOS, WIDTH), BF16),
            pltpu.VMEM((POINTS, WIDTH), BF16),
            pltpu.VMEM((PROTOS, WIDTH), BF16),
            pltpu.VMEM((GROUPS, 8, POINTS), F32),
            pltpu.VMEM((GROUPS, 8, POINTS), F32),
            pltpu.VMEM((ZH, BLOCK, POINTS), BF16),
            pltpu.VMEM((8, POINTS), F32),
            pltpu.VMEM((GROUPS, 8, 128), F32),
            pltpu.VMEM((8, POINTS), F32),
            pltpu.VMEM((GROUPS, 8, 128), F32),
            pltpu.VMEM((ROUNDS, Y, LANES, 128), F32),
            pltpu.VMEM((ROUNDS, ZL, LANES, 128), F32),
            pltpu.VMEM((ROUNDS, X * CORE, PROTOS // 128, 128), F32),
            pltpu.VMEM((ROUNDS, X * CORE, PROTOS // 128, 128), F32),
            pltpu.VMEM((ROUNDS, ZH, PROTOS // 128, 128), F32),
            pltpu.VMEM((ZH, THIRDS, X, CORE, OUT, 256), F32),
            pltpu.VMEM((ZH, THIRDS, X, OUT, 256), F32),
            pltpu.VMEM((ZH, THIRDS, X - 1, OUT, 256), F32),
            pltpu.VMEM((ZH, THIRDS, OUT, 256), F32),
            pltpu.VMEM((THIRDS, 2, HALF, 256), F32),
            pltpu.VMEM((THIRDS, 2, OUT, 256), F32),
            pltpu.VMEM((PROTOS // 128, 128), F32),
            dma((NCHUNK + 4,)),
            dma((ROUNDS, Y)), dma((ROUNDS, Y)),
            dma((ROUNDS, ZL)), dma((ROUNDS, ZL)),
            dma((ROUNDS, X * CORE)), dma((ROUNDS, X * CORE)),
            dma((ROUNDS, X * CORE)), dma((ROUNDS, X * CORE)),
            dma((ROUNDS, ZH)), dma((ROUNDS, ZH)),
            dma((ZH, THIRDS)), dma((ZH, THIRDS)),
            dma((ZH, THIRDS, X - 1)), dma((ZH, THIRDS, X - 1)),
            dma((THIRDS, 2)), dma((THIRDS, 2)),
            dma((THIRDS, 2, 2)), dma((THIRDS, 2, 2)),
        ],
        compiler_params=pltpu.CompilerParams(
            collective_id=0, has_side_effects=True, vmem_limit_bytes=56 * 1024 * 1024),
        name="assign",
    )(plan_stride_lengths, sigma_steps, points, prototypes)
    rows, cols, new = pl.pallas_call(
        results,
        out_shape=(
            jax.ShapeDtypeStruct((LANES, 128), F32),
            jax.ShapeDtypeStruct((PROTOS // 128, 128), F32),
            jax.ShapeDtypeStruct((OUT, WIDTH), F32),
        ),
        in_specs=[vmem, vmem, vmem],
        out_specs=(vmem, vmem, vmem),
        name="results",
    )(rows, cols, new)
    return rows.reshape(POINTS), cols.reshape(PROTOS), new


def solution(mesh):
    placed = (P("dp", None), P("proto", None), P(), P())
    return jax.shard_map(
        body,
        mesh=mesh,
        in_specs=placed,
        out_specs=(P("dp"), P("proto"), P(("proto", "dp"), None)),
        check_vma=False,
    )
```

```python
import jax
import jax.numpy as jnp
from jax import lax
from jax.experimental import pallas as pl
from jax.experimental.pallas import tpu as pltpu
from jax.sharding import PartitionSpec as P

K = 16384
SHARPNESS = 20.0
MESH = pl.DeviceIdType.MESH

ZH, X, CORE, ZL, Y = 4, 4, 2, 4, 4
ROUNDS = 3
POINTS, PROTOS, WIDTH = 2048, 1024, 768
PCHUNK = 512
NCHUNK = POINTS // PCHUNK
PHALF = PROTOS // 2
LANES = POINTS // 128
GROUPS = PROTOS // 8
BLOCK = PROTOS // ZH
BGROUPS = BLOCK // 8
OUT = PROTOS // (ZH * X * CORE)
HALF = OUT // 2
THIRDS = WIDTH // 256
F32, BF16 = jnp.float32, jnp.bfloat16


def unit_rows(values):
    wide = values.astype(F32)
    return (wide * lax.rsqrt(jnp.mean(wide * wide, axis=1, keepdims=True) + 1e-06)).astype(BF16)


def kernel(
    strides_hbm, sigmas_hbm, pts_hbm, protos_hbm,
    rowd_ref, cold_ref, newp_ref,
    strides, sigmas, pts, protos, upts, uprot, a_ref, b_ref, plan, wr, wc, rowacc, colacc,
    ra, rb, ca, cf, cb, part, corebuf, xbuf, total, zmid, zend, count_ref,
    in_sem, ra_s, ra_r, rb_s, rb_r, ca_s, ca_r, cf_s, cf_r, cb_s, cb_r, core_s, core_r, x_s, x_r, far_s, far_r, near_s, near_r,
):
    me_dp, me_pr = lax.axis_index("dp"), lax.axis_index("proto")
    zh, x, core = me_dp // (X * CORE), (me_dp // CORE) % X, me_dp % CORE
    xc = me_dp % (X * CORE)
    zl, y = me_pr // Y, me_pr % Y

    def at_xc(d):
        return (zh * (X * CORE) + d, me_pr)

    def at_x(d):
        return at_xc(((x + d + X) % X) * CORE + core)

    def at_zh(d):
        return (((zh + d + ZH) % ZH) * (X * CORE) + xc, me_pr)

    def at_y(d):
        return (me_dp, zl * Y + (y + d) % Y)

    def at_zl(d):
        return (me_dp, ((zl + d) % ZL) * Y + y)

    xc_peers = []
    for d in range(1, X * CORE):
        slot = ((x + d // CORE) % X) * CORE + (core + d % CORE) % CORE
        xc_peers.append((slot, at_xc(slot)))
    far_peers = []
    for d in range(X * CORE):
        slot = ((x + d // CORE) % X) * CORE + (core + d % CORE) % CORE
        far_peers.append((slot, (((zh + 2) % ZH) * (X * CORE) + slot, me_pr)))
    zh_peers = [((zh + d) % ZH, at_zh(d)) for d in (1, ZH - 1)]
    y_peers = [((y + d) % Y, at_y(d)) for d in range(1, Y)]
    zl_peers = [((zl + d) % ZL, at_zl(d)) for d in range(1, ZL)]
    everyone = xc_peers + far_peers + zh_peers + y_peers + zl_peers

    barrier = pltpu.get_barrier_semaphore()
    for _, dev in everyone:
        pl.semaphore_signal(barrier, inc=1, device_id=dev, device_id_type=MESH)

    def protos_in(h):
        rows = pl.ds(h * PHALF, PHALF)
        return pltpu.make_async_copy(protos_hbm.at[rows], protos.at[rows], in_sem.at[NCHUNK + h])

    def pts_in(j):
        rows = pl.ds(j * PCHUNK, PCHUNK)
        return pltpu.make_async_copy(pts_hbm.at[rows], pts.at[rows], in_sem.at[j])

    protos_in(0).start()
    for j in range(NCHUNK):
        pts_in(j).start()
    protos_in(1).start()
    strides_in = pltpu.make_async_copy(strides_hbm, strides, in_sem.at[NCHUNK + 2])
    sigmas_in = pltpu.make_async_copy(sigmas_hbm, sigmas, in_sem.at[NCHUNK + 3])
    strides_in.start()
    sigmas_in.start()

    scale = SHARPNESS / WIDTH
    target = float(POINTS * ZH * X * CORE) / K

    pending = []

    def spread(buf, send, recv, t, mine, peers):
        for slot, dev in peers:
            copy = pltpu.make_async_remote_copy(
                src_ref=buf.at[t, mine], dst_ref=buf.at[t, mine],
                send_sem=send.at[t, slot], recv_sem=recv.at[t, mine],
                device_id=dev, device_id_type=MESH)
            copy.start()
            pending.append(copy)

    def far_group(t, slot, dev):
        return pltpu.make_async_remote_copy(
            src_ref=ca.at[t, xc], dst_ref=cf.at[t, xc],
            send_sem=cf_s.at[t, slot], recv_sem=cf_r.at[t, xc],
            device_id=dev, device_id_type=MESH)

    def total_of(buf, t):
        out = buf[t, 0]
        for slot in range(1, buf.shape[1]):
            out = out + buf[t, slot]
        return out

    def gather(buf, send, recv, t, peers):
        for slot, dev in peers:
            pltpu.make_async_remote_copy(
                src_ref=buf.at[t, slot], dst_ref=buf.at[t, slot],
                send_sem=send.at[t, slot], recv_sem=recv.at[t, slot],
                device_id=dev, device_id_type=MESH).wait_recv()
        return total_of(buf, t)

    def sums_out(t, factor):
        for g in range(PROTOS // 128):
            block = colacc[g * 16:(g + 1) * 16].reshape(128, 128)
            ca[t, xc, g:g + 1, :] = factor * jnp.sum(block.T, axis=0, keepdims=True)
        for slot, dev in far_peers:
            copy = far_group(t, slot, dev)
            copy.start()
            pending.append(copy)
        spread(ca, ca_s, ca_r, t, xc, xc_peers)
        for l in range(LANES):
            ra[t, y, l:l + 1, :] = factor * jnp.sum(rowacc[:, l * 128:(l + 1) * 128], axis=0, keepdims=True)
        spread(ra, ra_s, ra_r, t, y, y_peers)

    def sums_mid(t):
        cb[t, zh] = gather(ca, ca_s, ca_r, t, xc_peers)
        spread(cb, cb_s, cb_r, t, zh, zh_peers)
        rb[t, zl] = gather(ra, ra_s, ra_r, t, y_peers)
        spread(rb, rb_s, rb_r, t, zl, zl_peers)

    def rows_in(t):
        return gather(rb, rb_s, rb_r, t, zl_peers)

    def cols_in(t):
        for slot, dev in far_peers:
            pltpu.make_async_remote_copy(
                src_ref=ca.at[t, xc], dst_ref=cf.at[t, slot],
                send_sem=cf_s.at[t, slot], recv_sem=cf_r.at[t, slot],
                device_id=dev, device_id_type=MESH).wait_recv()
        cb[t, (zh + 2) % ZH] = total_of(cf, t)
        return gather(cb, cb_s, cb_r, t, zh_peers)

    def rowd_in(rowd, step):
        for l in range(LANES):
            wr[:, l * 128:(l + 1) * 128] = jnp.broadcast_to(step * rowd[l:l + 1, :], (8, 128))

    def cold_in(cold, step):
        tall = (step * cold).T
        for g in range(PROTOS // 128):
            wc[g * 16:(g + 1) * 16] = jnp.broadcast_to(tall[:, g:g + 1], (128, 128)).reshape(16, 8, 128)

    strides_in.wait()
    sigmas_in.wait()
    tau = [strides[t] / K for t in range(ROUNDS)]
    colacc[...] = jnp.zeros_like(colacc)
    rowacc[...] = jnp.zeros_like(rowacc)

    def unit_protos(h):
        protos_in(h).wait()
        for i in range(PHALF // 128):
            rows = slice(h * PHALF + i * 128, h * PHALF + (i + 1) * 128)
            uprot[rows, :] = unit_rows(protos[rows, :])

    def unit_points(j):
        pts_in(j).wait()
        rows = slice(j * PCHUNK, (j + 1) * PCHUNK)
        upts[rows, :] = unit_rows(pts[rows, :])

    def scores(first, count, lanes, width):
        rows = pl.ds(pl.multiple_of(first, BLOCK), count)
        groups = pl.ds(first // 8, count // 8)
        s = lax.dot_general(uprot[rows, :], upts[lanes, :], (((1,), (1,)), ((), ())), preferred_element_type=F32)
        s = s.reshape(count // 8, 8, width)
        a_ref[groups, :, lanes] = s
        p = jnp.maximum(s, 0.0)
        rowacc[:, lanes] += jnp.sum(p, axis=0)
        acc = p[:, :, 0:128]
        for l in range(1, width // 128):
            acc = acc + p[:, :, l * 128:(l + 1) * 128]
        colacc[groups] += acc

    unit_protos(0)
    unit_points(0)
    for j in range(NCHUNK):
        scores(0, PHALF, slice(j * PCHUNK, (j + 1) * PCHUNK), PCHUNK)
        if j + 1 < NCHUNK:
            unit_points(j + 1)
    unit_protos(1)

    def rest(i, carry):
        scores(i * BLOCK, BLOCK, slice(0, POINTS), POINTS)
        return carry

    lax.fori_loop(PHALF // BLOCK, ZH, rest, 0)
    pl.semaphore_wait(barrier, len(everyone))

    def first_plan(i, carry):
        rows = pl.ds(i * 4, 4)
        s = a_ref[rows]
        b_ref[rows] = jnp.maximum((tau[1] * scale) * s, ((tau[0] + tau[1]) * scale) * s)
        return carry

    def next_plan(i, carry):
        rows = pl.ds(i * 4, 4)
        b_ref[rows] = b_ref[rows] + (tau[2] * scale) * a_ref[rows]
        return carry

    def iterate(base, count, store):
        def step(i, sums):
            rows = pl.ds(base + i * 8, 8)
            c = wc[rows]
            acc, out = None, []
            for l in range(LANES):
                lanes = slice(l * 128, (l + 1) * 128)
                p = jnp.maximum(b_ref[rows, :, lanes] - (wr[:, lanes] + c), 0.0)
                out.append(sums[l] + jnp.sum(p, axis=0))
                acc = p if acc is None else acc + p
                store(i, rows, lanes, p)
            colacc[rows] = acc
            return tuple(out)

        none = tuple(jnp.zeros((8, 128), F32) for _ in range(LANES))
        sums = lax.fori_loop(0, count, step, none)
        for l in range(LANES):
            rowacc[:, l * 128:(l + 1) * 128] += sums[l]

    sums_out(0, tau[0] * scale)
    lax.fori_loop(0, GROUPS // 8, first_plan, 0)
    sums_mid(0)
    lax.fori_loop(GROUPS // 8, GROUPS // 4, first_plan, 0)
    rowacc[...] = jnp.zeros_like(rowacc)
    rows1 = rows_in(0)
    rowd = sigmas[0] * (2.0 * rows1 - 1.0)
    rowd_in(rowd, tau[1])
    cols1 = cols_in(0)
    cold = sigmas[0] * (2.0 * cols1 - target)
    cold_in(cold, tau[1])


    def keep(i, rows, lanes, p):
        b_ref[rows, :, lanes] = p

    iterate(0, GROUPS // 8, keep)
    sums_out(1, 1.0)
    lax.fori_loop(0, GROUPS // 8, next_plan, 0)
    sums_mid(1)
    lax.fori_loop(GROUPS // 8, GROUPS // 4, next_plan, 0)
    rowacc[...] = jnp.zeros_like(rowacc)
    rows2 = rows_in(1)
    rowd = rowd + sigmas[1] * (2.0 * rows2 - rows1 - 1.0)
    rowd_in(rowd, tau[2])
    cols2 = cols_in(1)
    cold = cold + sigmas[1] * (2.0 * cols2 - cols1 - target)
    cold_in(cold, tau[2])

    other = 1 - core
    peer = at_xc(x * CORE + other)
    right, left, across = at_x(1), at_x(-1), at_x(2)
    up, down = at_zh(1), at_zh(-1)
    xp, xm, xo = (x + 1) % X, (x + X - 1) % X, (x + 2) % X
    lo, hi = pl.ds(0, HALF), pl.ds(HALF, HALF)

    def remote(src, dst, send, recv, index, dev):
        return pltpu.make_async_remote_copy(
            src_ref=src, dst_ref=dst, send_sem=send.at[index], recv_sem=recv.at[index],
            device_id=dev, device_id_type=MESH)

    def core_copy(c, h):
        return remote(part.at[c, h, :, other], corebuf.at[c, h], core_s, core_r, (c, h), peer)

    def x_copy(c, h, n):
        to, dev = ((xp, right), (xm, left), (xo, across))[n]
        return remote(part.at[c, h, to, core], xbuf.at[c, h, n], x_s, x_r, (c, h, n), dev)

    def far_copy(h, n):
        rows, dev = ((lo, up), (hi, down))[n]
        return remote(total.at[0, h, rows], zmid.at[h, n], far_s, far_r, (h, n), dev)

    def near_copy(h, n, second):
        rows = (lo, hi)[n if second else 1 - n]
        return remote(total.at[1 + n, h, rows], zend.at[h, n, rows], near_s, near_r, (h, n, int(second)), (up, down)[n])

    def over_h(step):
        def loop(h, carry):
            step(h)
            return carry

        lax.fori_loop(0, THIRDS, loop, 0)

    def x_out(c, h):
        core_copy(c, h).wait_recv()
        for n in (2, 0, 1):
            to = (xp, xm, xo)[n]
            part[c, h, to, core] += corebuf[c, h, to]
            x_copy(c, h, n).start()

    def x_in(c, h):
        for n in range(X - 1):
            x_copy(c, h, n).wait_recv()
        total[c, h] = part[c, h, x, core] + corebuf[c, h, x] + (xbuf[c, h, 0] + xbuf[c, h, 1] + xbuf[c, h, 2])

    def plan_block(c, carry):
        second, odd = c // 2, c % 2
        base = ((zh + 2 + second - odd + 2 * second * odd) % ZH) * BGROUPS

        def low(i, rows, lanes, p):
            plan[c, pl.ds(pl.multiple_of(i * 64, 64), 64), lanes] = p.reshape(64, 128).astype(BF16)

        iterate(base, BGROUPS // 8, low)
        return carry

    def third(c, h):
        lanes = pl.ds(pl.multiple_of(h * 256, 256), 256)
        g = jnp.dot(plan[c], pts[:, lanes], preferred_element_type=F32)
        part[c, h] = g.reshape(X, CORE, OUT, 256)
        core_copy(c, h).start()

    def sums_block(c, carry):
        over_h(lambda h: third(c, h))
        return carry

    lax.fori_loop(0, 1, plan_block, 0)
    lax.fori_loop(0, 1, sums_block, 0)
    lax.fori_loop(1, 2, plan_block, 0)
    x_out(0, 0)
    x_out(0, 1)
    lax.fori_loop(2, ZH, plan_block, 0)
    sums_out(2, 1.0)
    x_out(0, 2)
    lax.fori_loop(1, 3, sums_block, 0)
    x_out(1, 0)
    x_out(2, 0)
    x_out(1, 1)

    def far_out(h):
        x_in(0, h)
        for n in range(2):
            far_copy(h, n).start()
        x_out(2 - h % 2, 1 + (h + 1) // 2)
        third(3, h)

    over_h(far_out)
    sums_mid(2)

    def near_out(h):
        x_in(1, h)
        near_copy(h, 0, False).start()

        @pl.when(h < 2)
        def _():
            x_out(3, 2 * h)

        x_in(2, h)
        near_copy(h, 1, False).start()

        @pl.when(h == 0)
        def _():
            x_out(3, 1)

        for n in range(2):
            rows = (lo, hi)[n]
            far_copy(h, n).wait_recv()
            total[1 + n, h, rows] += zmid[h, n]
            near_copy(h, n, True).start()

    over_h(near_out)
    over_h(lambda h: x_in(3, h))
    rows3 = rows_in(2)
    cols3 = cols_in(2)
    rowd_ref[...] = rowd + sigmas[2] * (2.0 * rows3 - rows2 - 1.0)
    cold_ref[...] = cold + sigmas[2] * (2.0 * cols3 - cols2 - target)
    count_ref[...] = cols3
    mine = count_ref[pl.ds(me_dp // 4, 1), :]
    sub = lax.broadcasted_iota(jnp.int32, (OUT, 128), 0)
    lane = lax.broadcasted_iota(jnp.int32, (OUT, 128), 1)
    counts = jnp.sum(jnp.where(lane == sub + (me_dp % 4) * OUT, mine, 0.0), axis=1, keepdims=True)
    for h in range(THIRDS):
        lanes = slice(h * 256, (h + 1) * 256)
        for n in range(2):
            for second in (False, True):
                near_copy(h, n, second).wait_recv()
        gathered = total[3, h] + (zend[h, 0] + zend[h, 1])
        previous = protos[pl.ds(pl.multiple_of(me_dp * OUT, OUT), OUT), lanes].astype(F32)
        newp_ref[:, lanes] = (previous + gathered) / (1.0 + counts)

    def sent(h):
        def blocks(c, carry):
            core_copy(c, h).wait_send()
            for n in range(X - 1):
                x_copy(c, h, n).wait_send()
            return carry

        lax.fori_loop(0, ZH, blocks, 0)
        for n in range(2):
            far_copy(h, n).wait_send()
            near_copy(h, n, False).wait_send()
            near_copy(h, n, True).wait_send()

    over_h(sent)
    for copy in pending:
        copy.wait_send()


def results(rows_in, cols_in, new_in, rows_out, cols_out, new_out):
    rows_out[...] = rows_in[...]
    cols_out[...] = cols_in[...]
    new_out[...] = new_in[...]


def body(points, prototypes, plan_stride_lengths, sigma_steps):
    dma = pltpu.SemaphoreType.DMA
    vmem = pl.BlockSpec(memory_space=pltpu.VMEM)
    hbm = pl.BlockSpec(memory_space=pl.ANY)
    rows, cols, new = pl.pallas_call(
        kernel,
        out_shape=(
            pltpu.VMEM((LANES, 128), F32),
            pltpu.VMEM((PROTOS // 128, 128), F32),
            pltpu.VMEM((OUT, WIDTH), F32),
        ),
        in_specs=[hbm, hbm, hbm, hbm],
        out_specs=(vmem, vmem, vmem),
        scratch_shapes=[
            pltpu.SMEM((ROUNDS,), F32),
            pltpu.SMEM((ROUNDS,), F32),
            pltpu.VMEM((POINTS, WIDTH), BF16),
            pltpu.VMEM((PROTOS, WIDTH), BF16),
            pltpu.VMEM((POINTS, WIDTH), BF16),
            pltpu.VMEM((PROTOS, WIDTH), BF16),
            pltpu.VMEM((GROUPS, 8, POINTS), F32),
            pltpu.VMEM((GROUPS, 8, POINTS), F32),
            pltpu.VMEM((ZH, BLOCK, POINTS), BF16),
            pltpu.VMEM((8, POINTS), F32),
            pltpu.VMEM((GROUPS, 8, 128), F32),
            pltpu.VMEM((8, POINTS), F32),
            pltpu.VMEM((GROUPS, 8, 128), F32),
            pltpu.VMEM((ROUNDS, Y, LANES, 128), F32),
            pltpu.VMEM((ROUNDS, ZL, LANES, 128), F32),
            pltpu.VMEM((ROUNDS, X * CORE, PROTOS // 128, 128), F32),
            pltpu.VMEM((ROUNDS, X * CORE, PROTOS // 128, 128), F32),
            pltpu.VMEM((ROUNDS, ZH, PROTOS // 128, 128), F32),
            pltpu.VMEM((ZH, THIRDS, X, CORE, OUT, 256), F32),
            pltpu.VMEM((ZH, THIRDS, X, OUT, 256), F32),
            pltpu.VMEM((ZH, THIRDS, X - 1, OUT, 256), F32),
            pltpu.VMEM((ZH, THIRDS, OUT, 256), F32),
            pltpu.VMEM((THIRDS, 2, HALF, 256), F32),
            pltpu.VMEM((THIRDS, 2, OUT, 256), F32),
            pltpu.VMEM((PROTOS // 128, 128), F32),
            dma((NCHUNK + 4,)),
            dma((ROUNDS, Y)), dma((ROUNDS, Y)),
            dma((ROUNDS, ZL)), dma((ROUNDS, ZL)),
            dma((ROUNDS, X * CORE)), dma((ROUNDS, X * CORE)),
            dma((ROUNDS, X * CORE)), dma((ROUNDS, X * CORE)),
            dma((ROUNDS, ZH)), dma((ROUNDS, ZH)),
            dma((ZH, THIRDS)), dma((ZH, THIRDS)),
            dma((ZH, THIRDS, X - 1)), dma((ZH, THIRDS, X - 1)),
            dma((THIRDS, 2)), dma((THIRDS, 2)),
            dma((THIRDS, 2, 2)), dma((THIRDS, 2, 2)),
        ],
        compiler_params=pltpu.CompilerParams(
            collective_id=0, has_side_effects=True, vmem_limit_bytes=56 * 1024 * 1024),
        name="assign",
    )(plan_stride_lengths, sigma_steps, points, prototypes)
    rows, cols, new = pl.pallas_call(
        results,
        out_shape=(
            jax.ShapeDtypeStruct((LANES, 128), F32),
            jax.ShapeDtypeStruct((PROTOS // 128, 128), F32),
            jax.ShapeDtypeStruct((OUT, WIDTH), F32),
        ),
        in_specs=[vmem, vmem, vmem],
        out_specs=(vmem, vmem, vmem),
        compiler_params=pltpu.CompilerParams(vmem_limit_bytes=2 * 1024 * 1024),
        name="results",
    )(rows, cols, new)
    return rows.reshape(POINTS), cols.reshape(PROTOS), new


def solution(mesh):
    placed = (P("dp", None), P("proto", None), P(), P())
    return jax.shard_map(
        body,
        mesh=mesh,
        in_specs=placed,
        out_specs=(P("dp"), P("proto"), P(("proto", "dp"), None)),
        check_vma=False,
    )
```

```python
import jax
import jax.numpy as jnp
from jax import lax
from jax.experimental import pallas as pl
from jax.experimental.pallas import tpu as pltpu
from jax.sharding import PartitionSpec as P

K = 16384
SHARPNESS = 20.0
MESH = pl.DeviceIdType.MESH

ZH, X, CORE, ZL, Y = 4, 4, 2, 4, 4
ROUNDS = 3
POINTS, PROTOS, WIDTH = 2048, 1024, 768
PCHUNK = 512
NCHUNK = POINTS // PCHUNK
PFIRST = PROTOS * 3 // 4
LANES = POINTS // 128
GROUPS = PROTOS // 8
BLOCK = PROTOS // ZH
BGROUPS = BLOCK // 8
OUT = PROTOS // (ZH * X * CORE)
HALF = OUT // 2
THIRDS = WIDTH // 256
F32, BF16 = jnp.float32, jnp.bfloat16


def unit_rows(values):
    wide = values.astype(F32)
    return (wide * lax.rsqrt(jnp.mean(wide * wide, axis=1, keepdims=True) + 1e-06)).astype(BF16)


def kernel(
    strides_hbm, sigmas_hbm, pts_hbm, protos_hbm,
    rowd_ref, cold_ref, newp_ref,
    strides, sigmas, pts, protos, upts, uprot, a_ref, b_ref, plan, wr, wc, rowacc, colacc,
    ra, rb, ca, cf, cb, part, corebuf, xbuf, total, zmid, zend, count_ref,
    in_sem, ra_s, ra_r, rb_s, rb_r, ca_s, ca_r, cf_s, cf_r, cb_s, cb_r, core_s, core_r, x_s, x_r, far_s, far_r, near_s, near_r,
):
    me_dp, me_pr = lax.axis_index("dp"), lax.axis_index("proto")
    zh, x, core = me_dp // (X * CORE), (me_dp // CORE) % X, me_dp % CORE
    xc = me_dp % (X * CORE)
    zl, y = me_pr // Y, me_pr % Y

    def at_xc(d):
        return (zh * (X * CORE) + d, me_pr)

    def at_x(d):
        return at_xc(((x + d + X) % X) * CORE + core)

    def at_zh(d):
        return (((zh + d + ZH) % ZH) * (X * CORE) + xc, me_pr)

    def at_y(d):
        return (me_dp, zl * Y + (y + d) % Y)

    def at_zl(d):
        return (me_dp, ((zl + d) % ZL) * Y + y)

    xc_peers = []
    for d in range(1, X * CORE):
        slot = ((x + d // CORE) % X) * CORE + (core + d % CORE) % CORE
        xc_peers.append((slot, at_xc(slot)))
    far_peers = []
    for d in range(X * CORE):
        slot = ((x + d // CORE) % X) * CORE + (core + d % CORE) % CORE
        far_peers.append((slot, (((zh + 2) % ZH) * (X * CORE) + slot, me_pr)))
    zh_peers = [((zh + d) % ZH, at_zh(d)) for d in (1, ZH - 1)]
    y_peers = [((y + d) % Y, at_y(d)) for d in range(1, Y)]
    zl_peers = [((zl + d) % ZL, at_zl(d)) for d in range(1, ZL)]
    everyone = xc_peers + far_peers + zh_peers + y_peers + zl_peers

    barrier = pltpu.get_barrier_semaphore()
    for _, dev in everyone:
        pl.semaphore_signal(barrier, inc=1, device_id=dev, device_id_type=MESH)

    def protos_in(first, count, sem):
        rows = pl.ds(first, count)
        return pltpu.make_async_copy(protos_hbm.at[rows], protos.at[rows], in_sem.at[sem])

    protos_first = protos_in(0, PFIRST, NCHUNK)
    protos_rest = protos_in(PFIRST, PROTOS - PFIRST, NCHUNK + 1)

    def pts_in(j):
        rows = pl.ds(j * PCHUNK, PCHUNK)
        return pltpu.make_async_copy(pts_hbm.at[rows], pts.at[rows], in_sem.at[j])

    protos_first.start()
    for j in range(NCHUNK):
        pts_in(j).start()
    protos_rest.start()
    strides_in = pltpu.make_async_copy(strides_hbm, strides, in_sem.at[NCHUNK + 2])
    sigmas_in = pltpu.make_async_copy(sigmas_hbm, sigmas, in_sem.at[NCHUNK + 3])
    strides_in.start()
    sigmas_in.start()

    scale = SHARPNESS / WIDTH
    target = float(POINTS * ZH * X * CORE) / K

    pending = []

    def spread(buf, send, recv, t, mine, peers):
        for slot, dev in peers:
            copy = pltpu.make_async_remote_copy(
                src_ref=buf.at[t, mine], dst_ref=buf.at[t, mine],
                send_sem=send.at[t, slot], recv_sem=recv.at[t, mine],
                device_id=dev, device_id_type=MESH)
            copy.start()
            pending.append(copy)

    def far_group(t, slot, dev):
        return pltpu.make_async_remote_copy(
            src_ref=ca.at[t, xc], dst_ref=cf.at[t, xc],
            send_sem=cf_s.at[t, slot], recv_sem=cf_r.at[t, xc],
            device_id=dev, device_id_type=MESH)

    def total_of(buf, t):
        out = buf[t, 0]
        for slot in range(1, buf.shape[1]):
            out = out + buf[t, slot]
        return out

    def gather(buf, send, recv, t, peers):
        for slot, dev in peers:
            pltpu.make_async_remote_copy(
                src_ref=buf.at[t, slot], dst_ref=buf.at[t, slot],
                send_sem=send.at[t, slot], recv_sem=recv.at[t, slot],
                device_id=dev, device_id_type=MESH).wait_recv()
        return total_of(buf, t)

    def sums_out(t, factor):
        for g in range(PROTOS // 128):
            block = colacc[g * 16:(g + 1) * 16].reshape(128, 128)
            ca[t, xc, g:g + 1, :] = factor * jnp.sum(block.T, axis=0, keepdims=True)
        for slot, dev in far_peers:
            copy = far_group(t, slot, dev)
            copy.start()
            pending.append(copy)
        spread(ca, ca_s, ca_r, t, xc, xc_peers)
        for l in range(LANES):
            ra[t, y, l:l + 1, :] = factor * jnp.sum(rowacc[:, l * 128:(l + 1) * 128], axis=0, keepdims=True)
        spread(ra, ra_s, ra_r, t, y, y_peers)

    def sums_mid(t):
        cb[t, zh] = gather(ca, ca_s, ca_r, t, xc_peers)
        spread(cb, cb_s, cb_r, t, zh, zh_peers)
        rb[t, zl] = gather(ra, ra_s, ra_r, t, y_peers)
        spread(rb, rb_s, rb_r, t, zl, zl_peers)

    def rows_in(t):
        return gather(rb, rb_s, rb_r, t, zl_peers)

    def cols_in(t):
        for slot, dev in far_peers:
            pltpu.make_async_remote_copy(
                src_ref=ca.at[t, xc], dst_ref=cf.at[t, slot],
                send_sem=cf_s.at[t, slot], recv_sem=cf_r.at[t, slot],
                device_id=dev, device_id_type=MESH).wait_recv()
        cb[t, (zh + 2) % ZH] = total_of(cf, t)
        return gather(cb, cb_s, cb_r, t, zh_peers)

    def rowd_in(rowd, step):
        for l in range(LANES):
            wr[:, l * 128:(l + 1) * 128] = jnp.broadcast_to(step * rowd[l:l + 1, :], (8, 128))

    def cold_in(cold, step):
        tall = (step * cold).T
        for g in range(PROTOS // 128):
            wc[g * 16:(g + 1) * 16] = jnp.broadcast_to(tall[:, g:g + 1], (128, 128)).reshape(16, 8, 128)

    strides_in.wait()
    sigmas_in.wait()
    tau = [strides[t] / K for t in range(ROUNDS)]
    colacc[...] = jnp.zeros_like(colacc)
    rowacc[...] = jnp.zeros_like(rowacc)

    def unit_protos(copy, first, count):
        copy.wait()
        for i in range(count // 128):
            rows = slice(first + i * 128, first + (i + 1) * 128)
            uprot[rows, :] = unit_rows(protos[rows, :])

    def unit_points(j):
        pts_in(j).wait()
        rows = slice(j * PCHUNK, (j + 1) * PCHUNK)
        upts[rows, :] = unit_rows(pts[rows, :])

    def scores(first, count, lanes, width):
        rows = pl.ds(pl.multiple_of(first, BLOCK), count)
        groups = pl.ds(first // 8, count // 8)
        s = lax.dot_general(uprot[rows, :], upts[lanes, :], (((1,), (1,)), ((), ())), preferred_element_type=F32)
        s = s.reshape(count // 8, 8, width)
        a_ref[groups, :, lanes] = s
        p = jnp.maximum(s, 0.0)
        rowacc[:, lanes] += jnp.sum(p, axis=0)
        acc = p[:, :, 0:128]
        for l in range(1, width // 128):
            acc = acc + p[:, :, l * 128:(l + 1) * 128]
        colacc[groups] += acc

    unit_protos(protos_first, 0, PFIRST)
    unit_points(0)
    for j in range(NCHUNK):
        scores(0, PFIRST, slice(j * PCHUNK, (j + 1) * PCHUNK), PCHUNK)
        if j + 1 < NCHUNK:
            unit_points(j + 1)
    unit_protos(protos_rest, PFIRST, PROTOS - PFIRST)

    def rest(i, carry):
        scores(i * BLOCK, BLOCK, slice(0, POINTS), POINTS)
        return carry

    lax.fori_loop(PFIRST // BLOCK, ZH, rest, 0)
    pl.semaphore_wait(barrier, len(everyone))

    def first_plan(i, carry):
        rows = pl.ds(i * 4, 4)
        s = a_ref[rows]
        b_ref[rows] = jnp.maximum((tau[1] * scale) * s, ((tau[0] + tau[1]) * scale) * s)
        return carry

    def next_plan(i, carry):
        rows = pl.ds(i * 4, 4)
        b_ref[rows] = b_ref[rows] + (tau[2] * scale) * a_ref[rows]
        return carry

    def iterate(base, count, store):
        def step(i, sums):
            rows = pl.ds(base + i * 8, 8)
            c = wc[rows]
            acc, out = None, []
            for l in range(LANES):
                lanes = slice(l * 128, (l + 1) * 128)
                p = jnp.maximum(b_ref[rows, :, lanes] - (wr[:, lanes] + c), 0.0)
                out.append(sums[l] + jnp.sum(p, axis=0))
                acc = p if acc is None else acc + p
                store(i, rows, lanes, p)
            colacc[rows] = acc
            return tuple(out)

        none = tuple(jnp.zeros((8, 128), F32) for _ in range(LANES))
        sums = lax.fori_loop(0, count, step, none)
        for l in range(LANES):
            rowacc[:, l * 128:(l + 1) * 128] += sums[l]

    sums_out(0, tau[0] * scale)
    lax.fori_loop(0, GROUPS // 8, first_plan, 0)
    sums_mid(0)
    lax.fori_loop(GROUPS // 8, GROUPS // 4, first_plan, 0)
    rowacc[...] = jnp.zeros_like(rowacc)
    rows1 = rows_in(0)
    rowd = sigmas[0] * (2.0 * rows1 - 1.0)
    rowd_in(rowd, tau[1])
    cols1 = cols_in(0)
    cold = sigmas[0] * (2.0 * cols1 - target)
    cold_in(cold, tau[1])


    def keep(i, rows, lanes, p):
        b_ref[rows, :, lanes] = p

    iterate(0, GROUPS // 8, keep)
    sums_out(1, 1.0)
    lax.fori_loop(0, GROUPS // 8, next_plan, 0)
    sums_mid(1)
    lax.fori_loop(GROUPS // 8, GROUPS // 4, next_plan, 0)
    rowacc[...] = jnp.zeros_like(rowacc)
    rows2 = rows_in(1)
    rowd = rowd + sigmas[1] * (2.0 * rows2 - rows1 - 1.0)
    rowd_in(rowd, tau[2])
    cols2 = cols_in(1)
    cold = cold + sigmas[1] * (2.0 * cols2 - cols1 - target)
    cold_in(cold, tau[2])

    other = 1 - core
    peer = at_xc(x * CORE + other)
    right, left, across = at_x(1), at_x(-1), at_x(2)
    up, down = at_zh(1), at_zh(-1)
    xp, xm, xo = (x + 1) % X, (x + X - 1) % X, (x + 2) % X
    lo, hi = pl.ds(0, HALF), pl.ds(HALF, HALF)

    def remote(src, dst, send, recv, index, dev):
        return pltpu.make_async_remote_copy(
            src_ref=src, dst_ref=dst, send_sem=send.at[index], recv_sem=recv.at[index],
            device_id=dev, device_id_type=MESH)

    def core_copy(c, h):
        return remote(part.at[c, h, :, other], corebuf.at[c, h], core_s, core_r, (c, h), peer)

    def x_copy(c, h, n):
        to, dev = ((xp, right), (xm, left), (xo, across))[n]
        return remote(part.at[c, h, to, core], xbuf.at[c, h, n], x_s, x_r, (c, h, n), dev)

    def far_copy(h, n):
        rows, dev = ((lo, up), (hi, down))[n]
        return remote(total.at[0, h, rows], zmid.at[h, n], far_s, far_r, (h, n), dev)

    def near_copy(h, n, second):
        rows = (lo, hi)[n if second else 1 - n]
        return remote(total.at[1 + n, h, rows], zend.at[h, n, rows], near_s, near_r, (h, n, int(second)), (up, down)[n])

    def over_h(step):
        def loop(h, carry):
            step(h)
            return carry

        lax.fori_loop(0, THIRDS, loop, 0)

    def x_out(c, h):
        core_copy(c, h).wait_recv()
        for n in (2, 0, 1):
            to = (xp, xm, xo)[n]
            part[c, h, to, core] += corebuf[c, h, to]
            x_copy(c, h, n).start()

    def x_in(c, h):
        for n in range(X - 1):
            x_copy(c, h, n).wait_recv()
        total[c, h] = part[c, h, x, core] + corebuf[c, h, x] + (xbuf[c, h, 0] + xbuf[c, h, 1] + xbuf[c, h, 2])

    def plan_block(c, carry):
        second, odd = c // 2, c % 2
        base = ((zh + 2 + second - odd + 2 * second * odd) % ZH) * BGROUPS

        def low(i, rows, lanes, p):
            plan[c, pl.ds(pl.multiple_of(i * 64, 64), 64), lanes] = p.reshape(64, 128).astype(BF16)

        iterate(base, BGROUPS // 8, low)
        return carry

    def third(c, h):
        lanes = pl.ds(pl.multiple_of(h * 256, 256), 256)
        g = jnp.dot(plan[c], pts[:, lanes], preferred_element_type=F32)
        part[c, h] = g.reshape(X, CORE, OUT, 256)
        core_copy(c, h).start()

    def sums_block(c, carry):
        over_h(lambda h: third(c, h))
        return carry

    lax.fori_loop(0, 1, plan_block, 0)
    lax.fori_loop(0, 1, sums_block, 0)
    lax.fori_loop(1, 2, plan_block, 0)
    x_out(0, 0)
    x_out(0, 1)
    lax.fori_loop(2, ZH, plan_block, 0)
    sums_out(2, 1.0)
    x_out(0, 2)
    lax.fori_loop(1, 3, sums_block, 0)
    x_out(1, 0)
    x_out(2, 0)
    x_out(1, 1)

    def far_out(h):
        x_in(0, h)
        for n in range(2):
            far_copy(h, n).start()
        x_out(2 - h % 2, 1 + (h + 1) // 2)
        third(3, h)

    over_h(far_out)
    sums_mid(2)

    def near_out(h):
        x_in(1, h)
        near_copy(h, 0, False).start()

        @pl.when(h < 2)
        def _():
            x_out(3, 2 * h)

        x_in(2, h)
        near_copy(h, 1, False).start()

        @pl.when(h == 0)
        def _():
            x_out(3, 1)

        for n in range(2):
            rows = (lo, hi)[n]
            far_copy(h, n).wait_recv()
            total[1 + n, h, rows] += zmid[h, n]
            near_copy(h, n, True).start()

    over_h(near_out)
    over_h(lambda h: x_in(3, h))
    rows3 = rows_in(2)
    cols3 = cols_in(2)
    rowd_ref[...] = rowd + sigmas[2] * (2.0 * rows3 - rows2 - 1.0)
    cold_ref[...] = cold + sigmas[2] * (2.0 * cols3 - cols2 - target)
    count_ref[...] = cols3
    mine = count_ref[pl.ds(me_dp // 4, 1), :]
    sub = lax.broadcasted_iota(jnp.int32, (OUT, 128), 0)
    lane = lax.broadcasted_iota(jnp.int32, (OUT, 128), 1)
    counts = jnp.sum(jnp.where(lane == sub + (me_dp % 4) * OUT, mine, 0.0), axis=1, keepdims=True)
    for h in range(THIRDS):
        lanes = slice(h * 256, (h + 1) * 256)
        for n in range(2):
            for second in (False, True):
                near_copy(h, n, second).wait_recv()
        gathered = total[3, h] + (zend[h, 0] + zend[h, 1])
        previous = protos[pl.ds(pl.multiple_of(me_dp * OUT, OUT), OUT), lanes].astype(F32)
        newp_ref[:, lanes] = (previous + gathered) / (1.0 + counts)

    def sent(h):
        def blocks(c, carry):
            core_copy(c, h).wait_send()
            for n in range(X - 1):
                x_copy(c, h, n).wait_send()
            return carry

        lax.fori_loop(0, ZH, blocks, 0)
        for n in range(2):
            far_copy(h, n).wait_send()
            near_copy(h, n, False).wait_send()
            near_copy(h, n, True).wait_send()

    over_h(sent)
    for copy in pending:
        copy.wait_send()


def results(rows_in, cols_in, new_in, rows_out, cols_out, new_out):
    rows_out[...] = rows_in[...]
    cols_out[...] = cols_in[...]
    new_out[...] = new_in[...]


def body(points, prototypes, plan_stride_lengths, sigma_steps):
    dma = pltpu.SemaphoreType.DMA
    vmem = pl.BlockSpec(memory_space=pltpu.VMEM)
    hbm = pl.BlockSpec(memory_space=pl.ANY)
    rows, cols, new = pl.pallas_call(
        kernel,
        out_shape=(
            pltpu.VMEM((LANES, 128), F32),
            pltpu.VMEM((PROTOS // 128, 128), F32),
            pltpu.VMEM((OUT, WIDTH), F32),
        ),
        in_specs=[hbm, hbm, hbm, hbm],
        out_specs=(vmem, vmem, vmem),
        scratch_shapes=[
            pltpu.SMEM((ROUNDS,), F32),
            pltpu.SMEM((ROUNDS,), F32),
            pltpu.VMEM((POINTS, WIDTH), BF16),
            pltpu.VMEM((PROTOS, WIDTH), BF16),
            pltpu.VMEM((POINTS, WIDTH), BF16),
            pltpu.VMEM((PROTOS, WIDTH), BF16),
            pltpu.VMEM((GROUPS, 8, POINTS), F32),
            pltpu.VMEM((GROUPS, 8, POINTS), F32),
            pltpu.VMEM((ZH, BLOCK, POINTS), BF16),
            pltpu.VMEM((8, POINTS), F32),
            pltpu.VMEM((GROUPS, 8, 128), F32),
            pltpu.VMEM((8, POINTS), F32),
            pltpu.VMEM((GROUPS, 8, 128), F32),
            pltpu.VMEM((ROUNDS, Y, LANES, 128), F32),
            pltpu.VMEM((ROUNDS, ZL, LANES, 128), F32),
            pltpu.VMEM((ROUNDS, X * CORE, PROTOS // 128, 128), F32),
            pltpu.VMEM((ROUNDS, X * CORE, PROTOS // 128, 128), F32),
            pltpu.VMEM((ROUNDS, ZH, PROTOS // 128, 128), F32),
            pltpu.VMEM((ZH, THIRDS, X, CORE, OUT, 256), F32),
            pltpu.VMEM((ZH, THIRDS, X, OUT, 256), F32),
            pltpu.VMEM((ZH, THIRDS, X - 1, OUT, 256), F32),
            pltpu.VMEM((ZH, THIRDS, OUT, 256), F32),
            pltpu.VMEM((THIRDS, 2, HALF, 256), F32),
            pltpu.VMEM((THIRDS, 2, OUT, 256), F32),
            pltpu.VMEM((PROTOS // 128, 128), F32),
            dma((NCHUNK + 4,)),
            dma((ROUNDS, Y)), dma((ROUNDS, Y)),
            dma((ROUNDS, ZL)), dma((ROUNDS, ZL)),
            dma((ROUNDS, X * CORE)), dma((ROUNDS, X * CORE)),
            dma((ROUNDS, X * CORE)), dma((ROUNDS, X * CORE)),
            dma((ROUNDS, ZH)), dma((ROUNDS, ZH)),
            dma((ZH, THIRDS)), dma((ZH, THIRDS)),
            dma((ZH, THIRDS, X - 1)), dma((ZH, THIRDS, X - 1)),
            dma((THIRDS, 2)), dma((THIRDS, 2)),
            dma((THIRDS, 2, 2)), dma((THIRDS, 2, 2)),
        ],
        compiler_params=pltpu.CompilerParams(
            collective_id=0, has_side_effects=True, vmem_limit_bytes=56 * 1024 * 1024),
        name="assign",
    )(plan_stride_lengths, sigma_steps, points, prototypes)
    rows, cols, new = pl.pallas_call(
        results,
        out_shape=(
            jax.ShapeDtypeStruct((LANES, 128), F32),
            jax.ShapeDtypeStruct((PROTOS // 128, 128), F32),
            jax.ShapeDtypeStruct((OUT, WIDTH), F32),
        ),
        in_specs=[vmem, vmem, vmem],
        out_specs=(vmem, vmem, vmem),
        compiler_params=pltpu.CompilerParams(vmem_limit_bytes=2 * 1024 * 1024),
        name="results",
    )(rows, cols, new)
    return rows.reshape(POINTS), cols.reshape(PROTOS), new


def solution(mesh):
    placed = (P("dp", None), P("proto", None), P(), P())
    return jax.shard_map(
        body,
        mesh=mesh,
        in_specs=placed,
        out_specs=(P("dp"), P("proto"), P(("proto", "dp"), None)),
        check_vma=False,
    )
```
